256 devices in a mesh: ctx: 32 (over z, y), ep: 8 (over x, core).
Axes of the slice: x: 4, y: 4, z: 8, core: 2. Of those that a mesh axis runs over, the one named last changes fastest.
Arguments:
- tokens: bfloat16 [8, 8192, 2048], P('ep', 'ctx'), may hold values from -12 to 12
- queries: bfloat16 [8, 8192, 2048], P('ep', 'ctx'), may hold values from -100 to 100
- keys: bfloat16 [8, 8192, 256], P('ep', 'ctx'), may hold values from -4 to 4
- values: bfloat16 [8, 8192, 256], P('ep', 'ctx'), may hold values from -6 to 6
- lengths: int32 [8, 16], P('ep'), may hold values from 1 to 2048, 8192 in all within a row
- out_proj: bfloat16 [2048, 2048], P('ctx'), may hold values from -0.5 to 0.5
- norm_gain: float32 [2048], replicated, may hold values from 0.5 to 1.5
- expert_ids: int32 [8, 8192, 1], P('ep', 'ctx'), may hold values from 0 to 7; in each aligned block of 256 rows (0 to 255, 256 to 511, ..., all dimensions but the last counted through in order) at most 64 rows name the same one
- gate_prob: float32 [8, 8192, 1], P('ep', 'ctx'), may hold values from 0.2 to 1
- w_gate: bfloat16 [8, 2048, 768], P('ep'), may hold values from -0.125 to 0.125
- w_up: bfloat16 [8, 2048, 768], P('ep'), may hold values from -0.125 to 0.125
- w_down: bfloat16 [8, 768, 2048], P('ep'), may hold values from -0.21875 to 0.21875
Outputs:
- layer_out: bfloat16 [8, 8192, 2048], P('ep', 'ctx')
The draws below stay inside these ranges and needn't reach their ends.
Inputs may be any that keep to these rules, and one draw needn't show every extreme that they name: Each sequence's 16 lengths sum to 8192; the longest is exactly 2048. `expert_ids`: among the 256 tokens of one device at most 64 name the same expert, and in every draw some device has an expert named by exactly 64 of its tokens.
All inputs are finite; a program needn't handle non-finite values.
Results may differ from the reference program's by a relative error of at most 0.015.
Values may be sent and summed in bfloat16 or wider, within the bound.
No kernel may reach another device: no remote copies, remote signals or barrier semaphores. Data moves between devices by JAX's collectives and lax.ppermute only.
A program may use at most 128 MiB of HBM per device.

```python
import math
import jax
import jax.numpy as jnp
import numpy as np
from jax import lax

D = 2048
QUERY_HEADS = 16
KEY_VALUE_HEADS = 2
HEAD_SIZE = 128
FFE = 768
TOKENS_PER_PART = 256
NDOCS = 16
SEQUENCE_LENGTH = 8192
SEQUENCE_COUNT = 8
DOCUMENT_LIMIT = 2048
EXPERTS_IN = 8
CAP = 64
N_CTX = 32


def shared_basis(key):
    return jax.random.truncated_normal(jax.random.fold_in(key, 11), -4.0, 4.0, (SEQUENCE_COUNT, SEQUENCE_LENGTH, KEY_VALUE_HEADS, HEAD_SIZE), jnp.float32)


def draw_queries(key, part):
    key = jax.random.fold_in(key, 1)
    drawn_rows = jax.random.truncated_normal(key, -4.0, 4.0, (SEQUENCE_COUNT, SEQUENCE_LENGTH, QUERY_HEADS, HEAD_SIZE), jnp.float32)
    return drawn_rows.reshape(SEQUENCE_COUNT, SEQUENCE_LENGTH, QUERY_HEADS * HEAD_SIZE).astype(jnp.bfloat16)


def draw_keys(key, part):
    basis_matrix_rows = shared_basis(key)
    return basis_matrix_rows.reshape(SEQUENCE_COUNT, SEQUENCE_LENGTH, KEY_VALUE_HEADS * HEAD_SIZE).astype(jnp.bfloat16)


def draw_tokens(key, part):
    key = jax.random.fold_in(key, 3)
    first_key, column_key, row_key = jax.random.split(key, 3)
    columns = jnp.exp(jax.random.uniform(column_key, (1, 1, D), jnp.float32, math.log(0.1), math.log(1.0)))
    row_scale = jnp.exp(jax.random.uniform(row_key, (SEQUENCE_COUNT, SEQUENCE_LENGTH, 1), jnp.float32, math.log(0.3), math.log(3.0)))
    entries = jax.random.truncated_normal(first_key, -4.0, 4.0, (SEQUENCE_COUNT, SEQUENCE_LENGTH, D), jnp.float32)
    return (entries * columns * row_scale).astype(jnp.bfloat16)


def level_of(rng, extent, pieces, low, largest):
    def one(axis_at, blocks):
        heights = jax.random.uniform(jax.random.fold_in(jax.random.fold_in(rng, 6), axis_at), (blocks,), jnp.float32, low / len(pieces), largest / len(pieces))
        return jnp.repeat(jnp.exp(heights), extent[axis_at] // blocks).reshape((-1,) + (1,) * (len(extent) - axis_at - 1))

    loudness = one(*pieces[0])
    for cut in pieces[1:]:
        loudness = loudness * one(*cut)
    return loudness


def length_profile(amount, total, reach, slope):
    portions = [(1 << 20) // math.isqrt(standing ** slope) + 1 for standing in range(2, amount + 1)]
    surplus, holding = total - reach - (amount - 1), [1] * (amount - 1)
    while surplus > 0:
        movable = [i for i in range(amount - 1) if holding[i] < reach]
        whole, budget = sum([portions[i] for i in movable]), surplus
        for i in movable:
            addition = min(reach - holding[i], max(1, budget * portions[i] // whole), surplus)
            holding[i] = holding[i] + addition
            surplus = surplus - addition
    return np.array([reach] + holding)


def uneven(stream_key, amount, total, most, slope):
    if amount == 2:
        one = jax.random.randint(stream_key, (), max(1, total - most), min(most, total - 1) + 1)
        return jnp.stack([one, total - one])
    sizes = jnp.asarray(length_profile(amount, total, most, slope), jnp.int32)
    twos = (amount - 1) // 2
    giver, sink = sizes[1:1 + 2 * twos:2], sizes[2:2 + 2 * twos:2]
    slack = jnp.minimum(giver - 1, most - sink)
    moved = jax.random.randint(jax.random.fold_in(stream_key, 1), (twos,), 0, 1 << 20) % (slack + 1)
    sizes = sizes.at[1:1 + 2 * twos:2].set(giver - moved).at[2:2 + 2 * twos:2].set(sink + moved)
    return sizes[jax.random.permutation(jax.random.fold_in(stream_key, 2), amount)]


def deal_out(own_key, own, number, rows, amount, top, most, skew):
    sequence = jax.random.permutation(own_key, amount)
    heavy_load, ordinary = shares(amount, rows * top, most, skew, True), shares(amount, rows * top, most, skew, False)
    places = jnp.arange(amount)

    def named(tallies, offset_by):
        used = int((tallies > 0).sum())
        fixed = max(1, used // 4)
        passed = fixed + (places - fixed + offset_by * (used - fixed)) % max(1, amount - fixed)
        return jnp.zeros((amount,), jnp.int32).at[sequence[jnp.where(places < fixed, places, passed)]].set(jnp.asarray(tallies, jnp.int32))

    tallies = jnp.where(number % 4 == 0, named(heavy_load, number // 4), named(ordinary, number - number // 4 - 1))
    mixed = jax.random.permutation(jax.random.fold_in(own, 3), amount)
    giver, sink = mixed[0:amount // 2 * 2:2], mixed[1:amount // 2 * 2:2]
    slack = jnp.minimum(tallies[giver] - 1, most - tallies[sink]) // 2
    slack = jnp.where((giver == sequence[0]) | (sink == sequence[0]) | (tallies[sink] == 0), 0, jnp.maximum(slack, 0))
    passed = jax.random.randint(jax.random.fold_in(own, 4), (amount // 2,), 0, 1 << 20) % (slack + 1)
    tallies = tallies.at[giver].add(-passed).at[sink].add(passed)
    items = jnp.searchsorted(jnp.cumsum(tallies), jnp.arange(rows * top), side="right").astype(jnp.int32)
    grid = items.reshape(top, rows).T
    grid = grid[jax.random.permutation(jax.random.fold_in(own, 1), rows)]
    offset_by = jax.random.randint(jax.random.fold_in(own, 2), (rows, 1), 0, top)
    return jnp.take_along_axis(grid, (jnp.arange(top)[None, :] + offset_by) % top, axis=1)


def shares(count, total, reach, lean, full):
    loads = [(1 << 20) // math.isqrt(grade ** lean) + 1 for grade in range(1, count + 1)]
    largest = reach if full else min(reach, max(-(-total // count), total * loads[0] // sum(loads)))
    least = 1 if total - largest >= count - 1 else 0
    given, rest = [largest] + [least] * (count - 1), total - largest - least * (count - 1)
    while rest > 0:
        movable = [i for i in range(1, count) if given[i] < largest] or [i for i in range(1, count) if given[i] < reach]
        whole, budget = sum([loads[i] for i in movable]), rest
        for i in movable:
            more = min(reach - given[i], max(1, budget * loads[i] // whole), rest)
            given[i] = given[i] + more
            rest = rest - more
    return np.array(given)


def noise(key, dims, spread, reach, pieces=(), kind=jnp.bfloat16):
    drawn = spread * jax.random.normal(key, dims, jnp.float32)
    if pieces:
        drawn = drawn * level_of(key, dims, pieces, -0.22, 0.18)
    return jnp.clip(drawn, -reach, reach).astype(kind)


def setup_inputs(seed: int = 0) -> dict:
    arg_keys = jax.random.split(jax.random.key(seed), 13)
    tokens = draw_tokens(jax.random.fold_in(arg_keys[12], 71), 0)
    queries = draw_queries(jax.random.fold_in(arg_keys[12], 71), 0)
    keys = draw_keys(jax.random.fold_in(arg_keys[12], 71), 0)
    values = noise(arg_keys[3], (SEQUENCE_COUNT, SEQUENCE_LENGTH, KEY_VALUE_HEADS * HEAD_SIZE), 1.0, 6.0, ((0, 8), (1, 32)))
    lengths = jax.vmap(lambda own: uneven(own, NDOCS, SEQUENCE_LENGTH, DOCUMENT_LIMIT, 2))(jax.random.split(arg_keys[4], SEQUENCE_COUNT)).reshape((SEQUENCE_COUNT, NDOCS)).astype(jnp.int32)
    out_proj = noise(arg_keys[5], (D, D), HEAD_SIZE ** -0.5, 0.5, ((0, 32),))
    norm_gain = jnp.clip(1.0 + 0.1 * jax.random.normal(arg_keys[6], (D,), jnp.float32), 0.5, 1.5)
    expert_ids_keys = jax.random.split(jax.random.fold_in(arg_keys[7], 1), SEQUENCE_COUNT * SEQUENCE_LENGTH // TOKENS_PER_PART)
    expert_ids_turns = jax.random.permutation(jax.random.fold_in(arg_keys[7], 3), SEQUENCE_COUNT * SEQUENCE_LENGTH // TOKENS_PER_PART)
    expert_ids = jax.vmap(lambda own, number: deal_out(jax.random.fold_in(arg_keys[7], 2), own, number, TOKENS_PER_PART, EXPERTS_IN, 1, CAP, 2))(expert_ids_keys, expert_ids_turns).reshape((SEQUENCE_COUNT, SEQUENCE_LENGTH, 1))
    gate_prob = jnp.clip(0.2 + 0.8 * jax.random.uniform(arg_keys[8], (SEQUENCE_COUNT, SEQUENCE_LENGTH, 1), jnp.float32) ** level_of(arg_keys[8], (SEQUENCE_COUNT, SEQUENCE_LENGTH, 1), ((0, 8), (1, 32)), -0.2, 0.2), 0.2, 1.0)
    w_gate = noise(arg_keys[9], (EXPERTS_IN, D, FFE), D ** -0.5, 0.125, ((0, 8),))
    w_up = noise(arg_keys[10], (EXPERTS_IN, D, FFE), D ** -0.5, 0.125, ((0, 8),))
    w_down = noise(arg_keys[11], (EXPERTS_IN, FFE, D), FFE ** -0.5, 0.21875, ((0, 8),))
    return {"tokens": tokens, "queries": queries, "keys": keys, "values": values, "lengths": lengths, "out_proj": out_proj, "norm_gain": norm_gain, "expert_ids": expert_ids, "gate_prob": gate_prob, "w_gate": w_gate, "w_up": w_up, "w_down": w_down}


masked_value = -1e+30
norm_epsilon = 1e-06

def document_ids(positions, bounds):
    return lax.optimization_barrier(jnp.sum((positions[:, None] >= bounds[None, :]).astype(jnp.int32), axis=1, dtype=jnp.int32))

def reference(tokens, queries, keys, values, lengths, out_proj, norm_gain, expert_ids, gate_prob, w_gate, w_up, w_down):
    query_group_size = QUERY_HEADS // KEY_VALUE_HEADS
    score_scale = 1.0 / math.sqrt(HEAD_SIZE)
    block_count = SEQUENCE_LENGTH // TOKENS_PER_PART
    layer_window = DOCUMENT_LIMIT + TOKENS_PER_PART
    token_count = SEQUENCE_COUNT * SEQUENCE_LENGTH

    def one_sequence(inputs):
        query_seq, key_sequence, value_sequence, doc_lengths = inputs
        bounds = jnp.cumsum(doc_lengths, dtype=jnp.int32)
        key_padding = jnp.concatenate([jnp.zeros((DOCUMENT_LIMIT, KEY_VALUE_HEADS * HEAD_SIZE), key_sequence.dtype), key_sequence], axis=0)
        value_padding = jnp.concatenate([jnp.zeros((DOCUMENT_LIMIT, KEY_VALUE_HEADS * HEAD_SIZE), value_sequence.dtype), value_sequence], axis=0)

        def one_block(block_index):
            first_position = (block_index * TOKENS_PER_PART).astype(jnp.int32)
            query_tile_block = lax.dynamic_slice_in_dim(query_seq, first_position, TOKENS_PER_PART, 0).astype(jnp.float32)
            query_tile_block = query_tile_block.reshape(TOKENS_PER_PART, KEY_VALUE_HEADS, query_group_size, HEAD_SIZE)
            key_tile_block = lax.dynamic_slice_in_dim(key_padding, first_position, layer_window, 0).astype(jnp.float32).reshape(layer_window, KEY_VALUE_HEADS, HEAD_SIZE)
            value_tile_block = lax.dynamic_slice_in_dim(value_padding, first_position, layer_window, 0).astype(jnp.float32).reshape(layer_window, KEY_VALUE_HEADS, HEAD_SIZE)
            query_pos = first_position + jnp.arange(TOKENS_PER_PART, dtype=jnp.int32)
            key_pos = first_position - DOCUMENT_LIMIT + jnp.arange(layer_window, dtype=jnp.int32)
            visible = document_ids(query_pos, bounds)[:, None] == document_ids(key_pos, bounds)[None, :]
            visible = visible & (key_pos[None, :] <= query_pos[:, None]) & (key_pos[None, :] >= 0)
            scores = jnp.einsum('qhgd,khd->hgqk', query_tile_block, key_tile_block) * score_scale
            scores = jnp.where(visible[None, None], scores, masked_value)
            highest = lax.optimization_barrier(jnp.max(scores, axis=-1, keepdims=True))
            weights = jnp.exp(scores - highest)
            total = lax.optimization_barrier(jnp.sum(weights, axis=-1))
            rounded = lax.optimization_barrier(weights.astype(jnp.bfloat16)).astype(jnp.float32)
            mixed = jnp.einsum('hgqk,khd->qhgd', rounded, value_tile_block)
            mixed = mixed / total.transpose(2, 0, 1)[..., None]
            return mixed.reshape(TOKENS_PER_PART, QUERY_HEADS * HEAD_SIZE).astype(jnp.bfloat16)
        blocks = lax.map(one_block, jnp.arange(block_count).astype(jnp.int32))
        return blocks.reshape(SEQUENCE_LENGTH, QUERY_HEADS * HEAD_SIZE)
    attention = lax.map(one_sequence, (queries, keys, values, lengths))
    projected = jnp.dot(attention.reshape(token_count, D).astype(jnp.float32), out_proj.astype(jnp.float32))
    residual = (tokens.reshape(token_count, D).astype(jnp.float32) + projected).astype(jnp.bfloat16)
    residual_wide = residual.astype(jnp.float32)
    normed = residual_wide * lax.rsqrt(lax.optimization_barrier(jnp.mean(residual_wide * residual_wide, axis=-1, keepdims=True)) + norm_epsilon)
    normed = (normed * norm_gain.astype(jnp.float32)).astype(jnp.bfloat16)
    chosen = expert_ids.reshape(token_count)
    order = jnp.argsort(chosen, stable=True).astype(jnp.int32)
    counts = lax.optimization_barrier(jnp.sum((chosen[None, :] == jnp.arange(EXPERTS_IN, dtype=jnp.int32)[:, None]).astype(jnp.int32), axis=1, dtype=jnp.int32))
    starts = jnp.cumsum(counts, dtype=jnp.int32) - counts
    limit = SEQUENCE_COUNT * N_CTX * CAP
    order_pad = jnp.concatenate([order, jnp.full((limit,), token_count, jnp.int32)])

    def one_expert(expert):
        rows = lax.dynamic_slice_in_dim(order_pad, starts[expert], limit, 0)
        rows = jnp.where(jnp.arange(limit, dtype=jnp.int32) < counts[expert], rows, token_count).astype(jnp.int32)
        picked = jnp.take(normed, rows, axis=0, mode='fill', fill_value=0).astype(jnp.float32)
        gate_part = jnp.dot(picked, w_gate[expert].astype(jnp.float32))
        up_part = jnp.dot(picked, w_up[expert].astype(jnp.float32))
        hidden = (jax.nn.silu(gate_part) * up_part).astype(jnp.bfloat16)
        hidden = lax.optimization_barrier(hidden).astype(jnp.float32)
        result = jnp.dot(hidden, w_down[expert].astype(jnp.float32)).astype(jnp.bfloat16)
        return (rows, result)
    rows, results = lax.map(one_expert, jnp.arange(EXPERTS_IN).astype(jnp.int32))
    expert_out = jnp.zeros((token_count, D), jnp.bfloat16)
    expert_out = expert_out.at[rows.reshape(-1)].set(results.reshape(-1, D), mode='drop')
    layer_out = residual_wide + gate_prob.reshape(token_count, 1) * expert_out.astype(jnp.float32)
    return layer_out.astype(jnp.bfloat16).reshape(SEQUENCE_COUNT, SEQUENCE_LENGTH, D)
```

```python
import math

import jax
import jax.numpy as jnp
from jax import lax
from jax.experimental import pallas as pl
from jax.experimental.pallas import tpu as pltpu
from jax.sharding import PartitionSpec as P

HEAD = 128
CAP = 64
GROUP = 8

masked_value = -1e30
norm_epsilon = 1e-06
BF = jnp.bfloat16
F32 = jnp.float32


def call(body, out_shape, name, vmem_mb=48, **kw):
    return pl.pallas_call(
        body,
        out_shape=out_shape,
        name=name,
        compiler_params=pltpu.CompilerParams(vmem_limit_bytes=vmem_mb * 1024 * 1024),
        **kw,
    )


def dot(a, b, dims=((1,), (0,))):
    return lax.dot_general(a, b, (dims, ((), ())), preferred_element_type=F32)


def attention_body(info, start, q, own, recv, out, acc, run_max, run_sum):
    rows = q.shape[0]
    heads = q.shape[1] // HEAD
    kv_heads = own.shape[1] // (2 * HEAD)
    per = heads // kv_heads
    factor = math.log2(math.e) / math.sqrt(HEAD)
    block, pos_in_group, n_full, n_active = info[0], info[1], info[2], info[3]
    key_iota = lax.broadcasted_iota(jnp.int32, (rows, rows), 0)
    query_iota = lax.broadcasted_iota(jnp.int32, (rows, rows), 1)

    def step(load, key_start, first, masked):
        if masked:
            key_pos = key_iota + key_start
            seen = (key_pos >= start[...]) & (key_pos <= query_iota + block * rows)
        for g in range(kv_heads):
            k = load(slice(None), slice(g * HEAD, (g + 1) * HEAD))
            vt = load(slice(g * HEAD, (g + 1) * HEAD), slice(kv_heads * HEAD, kv_heads * HEAD + rows))
            for i in range(per):
                h = g * per + i
                s = dot(k, q[:, h * HEAD : (h + 1) * HEAD], ((1,), (1,)))
                if masked:
                    s = jnp.where(seen, s, masked_value)
                top = jnp.max(s, axis=0, keepdims=True)
                if not first:
                    old = run_max[h]
                    top = jnp.maximum(old, top)
                    scale = jnp.exp2((old - top) * factor)
                w = jnp.exp2((s - top) * factor)
                total = jnp.sum(w, axis=0, keepdims=True)
                mixed = dot(vt, w.astype(BF))
                if first:
                    run_sum[h] = total
                    acc[h] = mixed
                else:
                    run_sum[h] = run_sum[h] * scale + total
                    acc[h] = acc[h] * scale + mixed
                run_max[h] = top

    step(lambda a, b: own[a, b], block * rows, True, True)

    def other(d, masked):
        src = lax.rem(pos_in_group - d + 2 * GROUP, GROUP)
        step(lambda a, b: recv[src, a, b], (block - d) * rows, False, masked)

    def full(d, c):
        other(d, False)
        return c

    def part(d, c):
        other(d, True)
        return c

    lax.fori_loop(1, n_full, full, 0)
    lax.fori_loop(n_full, n_active, part, 0)
    for h in range(heads):
        out[:, h * HEAD : (h + 1) * HEAD] = (acc[h] / run_sum[h]).T.astype(BF)


def project_body(attn, w, tokens, gain, target, residual, outgoing, wide):
    t = pl.program_id(0)
    cols = w.shape[1]
    here = pl.ds(pl.multiple_of(t * cols, cols), cols)
    res = (tokens[:, here].astype(F32) + dot(attn[...], w[...])).astype(BF)
    residual[:, here] = res

    @pl.when(t == pl.num_programs(0) - 1)
    def _():
        x = residual[...].astype(F32)
        mean = jnp.mean(x * x, axis=-1, keepdims=True)
        wide[...] = (x * lax.rsqrt(mean + norm_epsilon) * gain[...]).astype(BF)
        slots = outgoing.shape[0]
        rows = residual.shape[0]
        pick = (lax.broadcasted_iota(jnp.int32, (slots, rows), 0) == target[...]).astype(BF)
        outgoing[...] = dot(pick, wide[...]).astype(BF)


def expert_body(x, w_gate, w_up, w_down, out, acc):
    t = pl.program_id(0)
    gate = dot(x[...], w_gate[...])
    up = dot(x[...], w_up[...])
    hidden = (gate / (1.0 + jnp.exp(-gate)) * up).astype(BF)
    part = dot(hidden, w_down[...])

    @pl.when(t == 0)
    def _():
        acc[...] = part

    @pl.when(t > 0)
    def _():
        acc[...] += part

    @pl.when(t == pl.num_programs(0) - 1)
    def _():
        out[...] = acc[...].astype(BF)


def combine_body(returned, residual, gate_prob, target, out):
    slots = returned.shape[0]
    rows = residual.shape[0]
    pick = (lax.broadcasted_iota(jnp.int32, (rows, slots), 1) == target[...]).astype(BF)
    back = dot(pick, returned[...])
    out[...] = (residual[...].astype(F32) + gate_prob[...] * back).astype(BF)


def on_device(
    tokens,
    queries,
    keys,
    values,
    lengths,
    out_proj,
    norm_gain,
    expert_ids,
    gate_prob,
    w_gate,
    w_up,
    w_down,
):
    rows = tokens.shape[1]
    width = tokens.shape[2]
    heads = queries.shape[2] // HEAD
    n_ctx = lax.axis_size("ctx")
    n_ep = lax.axis_size("ep")
    me = lax.axis_index("ctx")
    slot = lax.rem(me, GROUP)
    groups = [[g * GROUP + i for i in range(GROUP)] for g in range(n_ctx // GROUP)]

    pair = jnp.concatenate([keys[0], values[0].T], axis=1)
    behind = lax.ppermute(pair, "ctx", [(i, (i + GROUP) % n_ctx) for i in range(n_ctx)])
    ahead = jnp.arange(GROUP, dtype=jnp.int32)[:, None, None] > slot
    payload = jnp.where(ahead, pair[None], behind[None])
    recv = lax.all_to_all(payload, "ctx", 0, 0, axis_index_groups=groups)
    weight = lax.all_gather(out_proj, "ctx", axis=0, tiled=True)

    bounds = jnp.cumsum(lengths[0], dtype=jnp.int32)
    offsets = jnp.arange(rows, dtype=jnp.int32)
    pos = me * rows + offsets
    start = jnp.max(jnp.where(bounds[None, :] <= pos[:, None], bounds[None, :], 0), axis=1)
    n_active = me - start[0] // rows + 1
    n_full = me - (start[rows - 1] + rows - 1) // rows + 1
    n_full = jnp.clip(n_full, 1, n_active)
    info = jnp.stack([me, slot, n_full, n_active]).astype(jnp.int32)

    smem = pl.BlockSpec(memory_space=pltpu.SMEM)
    vmem = pl.BlockSpec(memory_space=pltpu.VMEM)
    attn = call(
        attention_body,
        jax.ShapeDtypeStruct((rows, width), BF),
        "attention",
        in_specs=[smem, vmem, vmem, vmem, vmem],
        out_specs=vmem,
        scratch_shapes=[
            pltpu.VMEM((heads, HEAD, rows), F32),
            pltpu.VMEM((heads, 1, rows), F32),
            pltpu.VMEM((heads, 1, rows), F32),
        ],
    )(info, start[None, :], queries[0], pair, recv)

    chosen = expert_ids[0, :, 0]
    n_experts = w_gate.shape[0] * n_ep
    slots = n_experts * CAP
    onehot = (chosen[:, None] == jnp.arange(n_experts, dtype=jnp.int32)[None, :]).astype(jnp.int32)
    before = jnp.cumsum(onehot, axis=0, dtype=jnp.int32) - onehot
    target = chosen * CAP + jnp.sum(before * onehot, axis=1, dtype=jnp.int32)

    tile = 256
    residual, outgoing = call(
        project_body,
        (jax.ShapeDtypeStruct((rows, width), BF), jax.ShapeDtypeStruct((slots, width), BF)),
        "project",
        grid=(width // tile,),
        in_specs=[
            pl.BlockSpec((rows, width), lambda t: (0, 0)),
            pl.BlockSpec((width, tile), lambda t: (0, t)),
            pl.BlockSpec((rows, width), lambda t: (0, 0)),
            pl.BlockSpec((1, width), lambda t: (0, 0)),
            pl.BlockSpec((1, rows), lambda t: (0, 0)),
        ],
        out_specs=(
            pl.BlockSpec((rows, width), lambda t: (0, 0)),
            pl.BlockSpec((slots, width), lambda t: (0, 0)),
        ),
        scratch_shapes=[pltpu.VMEM((rows, width), BF)],
    )(attn, weight, tokens[0], norm_gain[None, :], target[None, :])

    incoming = lax.all_to_all(outgoing.reshape(n_ep, slots // n_ep, width), "ep", 0, 0)
    incoming = incoming.reshape(slots, width)
    ffe = w_gate.shape[2]
    expert_out = call(
        expert_body,
        jax.ShapeDtypeStruct((slots, width), BF),
        "experts",
        grid=(ffe // tile,),
        in_specs=[
            pl.BlockSpec((slots, width), lambda t: (0, 0)),
            pl.BlockSpec((width, tile), lambda t: (0, t)),
            pl.BlockSpec((width, tile), lambda t: (0, t)),
            pl.BlockSpec((tile, width), lambda t: (t, 0)),
        ],
        out_specs=pl.BlockSpec((slots, width), lambda t: (0, 0)),
        scratch_shapes=[pltpu.VMEM((slots, width), F32)],
    )(incoming, w_gate[0], w_up[0], w_down[0])
    returned = lax.all_to_all(expert_out.reshape(n_ep, slots // n_ep, width), "ep", 0, 0)
    returned = returned.reshape(slots, width)

    layer_out = call(
        combine_body,
        jax.ShapeDtypeStruct((rows, width), BF),
        "combine",
        in_specs=[vmem, vmem, vmem, vmem],
        out_specs=vmem,
    )(returned, residual, gate_prob[0], target[:, None])
    return layer_out[None]


def solution(mesh):
    placed = (
        P("ep", "ctx", None),
        P("ep", "ctx", None),
        P("ep", "ctx", None),
        P("ep", "ctx", None),
        P("ep", None),
        P("ctx", None),
        P(),
        P("ep", "ctx", None),
        P("ep", "ctx", None),
        P("ep", None, None),
        P("ep", None, None),
        P("ep", None, None),
    )
    return jax.shard_map(
        on_device, mesh=mesh, in_specs=placed, out_specs=P("ep", "ctx", None), check_vma=False
    )
```

```python
import math

import jax
import jax.numpy as jnp
from jax import lax
from jax.experimental import pallas as pl
from jax.experimental.pallas import tpu as pltpu
from jax.sharding import PartitionSpec as P

HEAD = 128
CAP = 64
KV_HEADS = 2
Y_SIZE = 4
Z_SIZE = 8
Z_RING = (0, 1, 2, 3, -1, -2, -3, -4)
EXTRA = 16
TOGETHER = 4

masked_value = -1e30
norm_epsilon = 1e-06
BF = jnp.bfloat16
F32 = jnp.float32


def call(body, out_shape, name, vmem_mb=48, **kw):
    return pl.pallas_call(
        body,
        out_shape=out_shape,
        name=name,
        compiler_params=pltpu.CompilerParams(vmem_limit_bytes=vmem_mb * 1024 * 1024),
        **kw,
    )


def cost(flops, size):
    return pl.CostEstimate(flops=int(flops), bytes_accessed=int(size), transcendentals=0)


def dot(a, b, dims=((1,), (0,))):
    return lax.dot_general(a, b, (dims, ((), ())), preferred_element_type=F32)


def attention_steps(info, start, q, acc, run_max):
    rows = q.shape[0]
    heads = q.shape[1] // HEAD
    per = heads // KV_HEADS
    factor = math.log2(math.e) / math.sqrt(HEAD)
    block = info[0]
    key_iota = lax.broadcasted_iota(jnp.int32, (rows, rows), 0)
    query_iota = lax.broadcasted_iota(jnp.int32, (rows, rows), 1)
    ones = jnp.ones((EXTRA, rows), BF)

    def step(load, d, first, masked):
        if masked:
            key_pos = key_iota + (block - d) * rows
            seen = (key_pos >= start[...]) & (key_pos <= query_iota + block * rows)
        ks = [load(slice(None), slice(g * HEAD, (g + 1) * HEAD)) for g in range(KV_HEADS)]
        vts = [
            jnp.concatenate([load(slice(g * HEAD, (g + 1) * HEAD), slice(KV_HEADS * HEAD, None)), ones], axis=0)
            for g in range(KV_HEADS)
        ]

        def score(hs):
            return [dot(ks[h // per], q[:, h * HEAD : (h + 1) * HEAD], ((1,), (1,))) for h in hs]

        def weigh(hs, ss):
            if masked:
                ss = [jnp.where(seen, s, masked_value) for s in ss]
            tops = [jnp.max(s, axis=0, keepdims=True) for s in ss]
            scales = None
            if not first:
                olds = [run_max[h] for h in hs]
                tops = [jnp.maximum(a, b) for a, b in zip(olds, tops)]
                scales = [jnp.exp2((a - b) * factor) for a, b in zip(olds, tops)]
            ws = [jnp.exp2((s - t) * factor).astype(BF) for s, t in zip(ss, tops)]
            for h, t in zip(hs, tops):
                run_max[h] = t
            return ws, scales

        def mix(hs, ws, scales):
            parts = [dot(vts[h // per], w) for h, w in zip(hs, ws)]
            for n, h in enumerate(hs):
                acc[h] = parts[n] if first else acc[h] * scales[n] + parts[n]

        sets = [list(range(a, a + TOGETHER)) for a in range(0, heads, TOGETHER)]
        ss = score(sets[0])
        waiting = None
        for n, hs in enumerate(sets):
            following = score(sets[n + 1]) if n + 1 < len(sets) else None
            weighed = weigh(hs, ss)
            if waiting is not None:
                mix(*waiting)
            waiting = (hs, *weighed)
            ss = following
        mix(*waiting)

    return step


def near_body(info, start, q, own, one_up, two_up, acc, run_max):
    step = attention_steps(info, start, q, acc, run_max)
    step(lambda a, b: own[a, b], 0, True, True)
    for d, ref in ((Y_SIZE, one_up), (2 * Y_SIZE, two_up)):

        @pl.when(d < info[3])
        def _():
            step(lambda a, b: ref[a, b], d, False, True)


def far_body(info, start, q, recv, acc_in, max_in, out, acc, run_max):
    heads = q.shape[1] // HEAD
    acc[...] = acc_in[...]
    run_max[...] = max_in[...]
    step = attention_steps(info, start, q, acc, run_max)

    def other(d, masked):
        src = lax.rem(info[1] - d + 4 * Y_SIZE, Y_SIZE)
        layer = lax.div(d - 1, Y_SIZE)

        @pl.when(lax.rem(d, Y_SIZE) != 0)
        def _():
            step(lambda a, b: recv[src, layer, a, b], d, False, masked)

    def full(d, c):
        other(d, False)
        return c

    def part(d, c):
        other(d, True)
        return c

    lax.fori_loop(1, info[2], full, 0)
    lax.fori_loop(info[2], info[3], part, 0)
    for h in range(heads):
        state = acc[h]
        out[:, h * HEAD : (h + 1) * HEAD] = (state[:HEAD] / state[HEAD : HEAD + 1]).T.astype(BF)


def project_body(place, attn, *refs):
    own_pieces = refs[: len(Z_RING)]
    other_pieces = refs[len(Z_RING) : 2 * len(Z_RING)]
    tokens, gain, target, residual = refs[2 * len(Z_RING) : 2 * len(Z_RING) + 4]
    outgoing = refs[2 * len(Z_RING) + 4 : -2]
    w, sems = refs[-2:]
    z, y = place[0], place[1]
    own = lax.rem(place[2], 2)
    halves = ((own, own_pieces), (1 - own, other_pieces))
    for n, (half, pieces) in enumerate(halves):
        for piece, dz in zip(pieces, Z_RING):
            for dy in range(Y_SIZE):
                z_at = lax.rem(z - dz + 2 * Z_SIZE, Z_SIZE)
                y_at = lax.rem(y - dy + Y_SIZE, Y_SIZE)
                pltpu.make_async_copy(piece.at[dy], w.at[half, z_at, y_at], sems.at[n]).start()
    rows, width = attn.shape
    cols = w.shape[-1]
    tile = 256
    for n, (half, _) in enumerate(halves):
        pltpu.make_async_copy(w.at[half], w.at[half], sems.at[n]).wait()
        for j in range(cols // tile):
            here = pl.ds(pl.multiple_of(half * cols + j * tile, tile), tile)
            weight = w[half, :, :, :, j * tile : (j + 1) * tile].reshape(width, tile)
            residual[:, here] = (tokens[:, here].astype(F32) + dot(attn[...], weight)).astype(BF)
    x = residual[...].astype(F32)
    mean = jnp.mean(x * x, axis=-1, keepdims=True)
    normed = (x * lax.rsqrt(mean + norm_epsilon) * gain[...]).astype(BF)
    for s, ref in enumerate(outgoing):
        slots = ref.shape[0]
        pick = (lax.broadcasted_iota(jnp.int32, (slots, rows), 0) + s * slots == target[...]).astype(BF)
        ref[...] = dot(pick, normed).astype(BF)


def expert_body(count, *refs):
    xs, (w_gate, w_up, w_down) = refs[:count], refs[count : count + 3]
    outs, (x, acc) = refs[count + 3 : 2 * count + 3], refs[2 * count + 3 :]
    t = pl.program_id(0)
    cap = xs[0].shape[0]

    @pl.when(t == 0)
    def _():
        for i, ref in enumerate(xs):
            x[i * cap : (i + 1) * cap, :] = ref[...]

    gate = dot(x[...], w_gate[...])
    up = dot(x[...], w_up[...])
    hidden = (gate / (1.0 + jnp.exp(-gate)) * up).astype(BF)
    part = dot(hidden, w_down[...])

    @pl.when(t == 0)
    def _():
        acc[...] = part

    @pl.when(t > 0)
    def _():
        acc[...] += part

    @pl.when(t == pl.num_programs(0) - 1)
    def _():
        for i, ref in enumerate(outs):
            ref[...] = acc[i * cap : (i + 1) * cap, :].astype(BF)


def combine_body(*refs):
    returned = refs[:-4]
    residual, gate_prob, target, out = refs[-4:]
    rows = residual.shape[0]
    slots = returned[0].shape[0]
    back = None
    for s in range(0, len(returned), 4):
        four = jnp.concatenate([r[...] for r in returned[s : s + 4]], axis=0)
        pick = (lax.broadcasted_iota(jnp.int32, (rows, 4 * slots), 1) + s * slots == target[...]).astype(BF)
        part = dot(pick, four)
        back = part if back is None else back + part
    out[...] = (residual[...].astype(F32) + gate_prob[...] * back).astype(BF)


def on_device(
    tokens,
    queries,
    keys,
    values,
    lengths,
    out_proj,
    norm_gain,
    expert_ids,
    gate_prob,
    w_gate,
    w_up,
    w_down,
):
    rows = tokens.shape[1]
    width = tokens.shape[2]
    heads = queries.shape[2] // HEAD
    n_ctx = lax.axis_size("ctx")
    n_ep = lax.axis_size("ep")
    me = lax.axis_index("ctx")
    y, z = lax.rem(me, Y_SIZE), lax.div(me, Y_SIZE)
    part = lax.axis_index("ep")
    y_groups = [[a * Y_SIZE + b for b in range(Y_SIZE)] for a in range(n_ctx // Y_SIZE)]

    def y_shift(array, by):
        return lax.ppermute(
            array, "ctx", [(a * Y_SIZE + b, a * Y_SIZE + (b + by) % Y_SIZE) for a in range(Z_SIZE) for b in range(Y_SIZE)]
        )

    def z_shift(array, by):
        return lax.ppermute(array, "ctx", [(i, (i + by * Y_SIZE) % n_ctx) for i in range(n_ctx)])

    def core_swap(array):
        return lax.ppermute(array, "ep", [(i, i ^ 1) for i in range(n_ep)])

    pair = jnp.concatenate([keys[0], values[0].T], axis=1)
    half = width // 2
    out_proj, pair = lax.optimization_barrier((out_proj, pair))
    mine = lax.dynamic_slice_in_dim(out_proj, lax.rem(part, 2) * half, half, 1)
    row = jnp.stack([mine] + [y_shift(mine, s) for s in range(1, Y_SIZE)])
    up, down = [row], [row]
    for _ in range(2):
        up.append(z_shift(up[-1], 1))
        down.append(z_shift(down[-1], -1))

    one_up = z_shift(pair, 1)
    two_up = z_shift(one_up, 1)
    to_after = jnp.arange(Y_SIZE, dtype=jnp.int32)[:, None, None, None] > y
    payload = jnp.where(to_after, jnp.stack([pair, one_up])[None], jnp.stack([one_up, two_up])[None])
    recv = lax.all_to_all(payload, "ctx", 0, 0, axis_index_groups=y_groups)

    bounds = jnp.cumsum(lengths[0], dtype=jnp.int32)
    offsets = jnp.arange(rows, dtype=jnp.int32)
    pos = me * rows + offsets
    start = jnp.max(jnp.where(bounds[None, :] <= pos[:, None], bounds[None, :], 0), axis=1)
    n_active = me - start[0] // rows + 1
    n_full = me - (start[rows - 1] + rows - 1) // rows + 1
    n_full = jnp.clip(n_full, 1, n_active)
    info = jnp.stack([me, y, n_full, n_active]).astype(jnp.int32)
    place = jnp.stack([z, y, part]).astype(jnp.int32)

    smem = pl.BlockSpec(memory_space=pltpu.SMEM)
    vmem = pl.BlockSpec(memory_space=pltpu.VMEM)
    anywhere = pl.BlockSpec(memory_space=pl.ANY)
    state = (
        jax.ShapeDtypeStruct((heads, HEAD + EXTRA, rows), F32),
        jax.ShapeDtypeStruct((heads, 1, rows), F32),
    )
    scratch = [pltpu.VMEM(s.shape, s.dtype) for s in state]
    acc, run_max = call(
        near_body,
        state,
        "near",
        in_specs=[smem] + [vmem] * 5,
        out_specs=(vmem, vmem),
        cost_estimate=cost(6e9, 6e6),
    )(info, start[None, :], queries[0], pair, one_up, two_up)
    held_up, held_down, run_max = lax.optimization_barrier((up[-1], down[-1], run_max))
    up.append(z_shift(held_up, 1))
    down.append(z_shift(held_down, -1))
    down.append(z_shift(down[-1], -1))
    own_pieces = up + down[1:]
    other_pieces = [core_swap(piece) for piece in own_pieces]
    attn = call(
        far_body,
        jax.ShapeDtypeStruct((rows, width), BF),
        "far",
        in_specs=[smem] + [vmem] * 5,
        out_specs=vmem,
        scratch_shapes=scratch,
        cost_estimate=cost(12e9, 6e6),
    )(info, start[None, :], queries[0], recv, acc, run_max)

    chosen = expert_ids[0, :, 0]
    n_experts = w_gate.shape[0] * n_ep
    onehot = (chosen[:, None] == jnp.arange(n_experts, dtype=jnp.int32)[None, :]).astype(jnp.int32)
    before = jnp.cumsum(onehot, axis=0, dtype=jnp.int32) - onehot
    target = (chosen ^ part) * CAP + jnp.sum(before * onehot, axis=1, dtype=jnp.int32)

    chunk = jax.ShapeDtypeStruct((CAP, width), BF)
    n_pieces = len(own_pieces)
    residual, *outgoing = call(
        project_body,
        (jax.ShapeDtypeStruct((rows, width), BF),) + (chunk,) * n_ep,
        "project",
        in_specs=[smem, vmem] + [anywhere] * (2 * n_pieces) + [vmem] * 3,
        out_specs=(vmem,) * (1 + n_ep),
        scratch_shapes=[
            pltpu.VMEM((2, Z_SIZE, Y_SIZE, out_proj.shape[0], half), BF),
            pltpu.SemaphoreType.DMA((2,)),
        ],
        cost_estimate=cost(2.6e9, 1.4e7),
    )(place, attn, *own_pieces, *other_pieces, tokens[0], norm_gain[None, :], target[None, :])

    def partner(array, s):
        return lax.ppermute(array, "ep", [(i, i ^ s) for i in range(n_ep)])

    tile = 256

    def experts(xs, name):
        n = len(xs)
        return call(
            lambda *refs: expert_body(n, *refs),
            (chunk,) * n,
            name,
            grid=(w_gate.shape[2] // tile,),
            in_specs=[pl.BlockSpec((CAP, width), lambda t: (0, 0))] * n
            + [pl.BlockSpec((width, tile), lambda t: (0, t))] * 2
            + [pl.BlockSpec((tile, width), lambda t: (t, 0))],
            out_specs=(pl.BlockSpec((CAP, width), lambda t: (0, 0)),) * n,
            scratch_shapes=[pltpu.VMEM((n * CAP, width), BF), pltpu.VMEM((n * CAP, width), F32)],
            cost_estimate=cost(n * CAP * 6 * width * w_gate.shape[2], 1e7),
        )(*xs, w_gate[0], w_up[0], w_down[0])

    near_set, far_set = (2, 3, 6, 7, 1), (4, 5)
    incoming = {s: partner(outgoing[s], s) for s in near_set + far_set}
    incoming[0] = outgoing[0]
    answers = dict(zip((0,) + near_set, experts([incoming[s] for s in (0,) + near_set], "experts_near")))
    answers.update(zip(far_set, experts([incoming[s] for s in far_set], "experts_far")))
    returned = [answers[0] if s == 0 else partner(answers[s], s) for s in range(n_ep)]

    layer_out = call(
        combine_body,
        jax.ShapeDtypeStruct((rows, width), BF),
        "combine",
        in_specs=[vmem] * (n_ep + 3),
        out_specs=vmem,
    )(*returned, residual, gate_prob[0], target[:, None])
    return layer_out[None]


def solution(mesh):
    placed = (
        P("ep", "ctx", None),
        P("ep", "ctx", None),
        P("ep", "ctx", None),
        P("ep", "ctx", None),
        P("ep", None),
        P("ctx", None),
        P(),
        P("ep", "ctx", None),
        P("ep", "ctx", None),
        P("ep", None, None),
        P("ep", None, None),
        P("ep", None, None),
    )
    return jax.shard_map(
        on_device, mesh=mesh, in_specs=placed, out_specs=P("ep", "ctx", None), check_vma=False
    )
```

```python
import math

import jax
import jax.numpy as jnp
from jax import lax
from jax.experimental import pallas as pl
from jax.experimental.pallas import tpu as pltpu
from jax.sharding import PartitionSpec as P

HEAD = 128
CAP = 64
KV_HEADS = 2
Y_SIZE = 4
Z_SIZE = 8
ALL_Y = (0, 1, 2, 3)
PIECES = tuple((dz, ALL_Y) for dz in (0, 1, 2, 3, -1, -2, -3)) + ((4, ALL_Y[:2]), (-4, ALL_Y[2:]))
EXTRA = 16
TOGETHER = 4

masked_value = -1e30
norm_epsilon = 1e-06
BF = jnp.bfloat16
F32 = jnp.float32


def call(body, out_shape, name, vmem_mb=48, **kw):
    return pl.pallas_call(
        body,
        out_shape=out_shape,
        name=name,
        compiler_params=pltpu.CompilerParams(vmem_limit_bytes=vmem_mb * 1024 * 1024),
        **kw,
    )


def cost(flops, size):
    return pl.CostEstimate(flops=int(flops), bytes_accessed=int(size), transcendentals=0)


def dot(a, b, dims=((1,), (0,))):
    return lax.dot_general(a, b, (dims, ((), ())), preferred_element_type=F32)


def document_starts(lengths, pos):
    end, start = 0, jnp.zeros_like(pos)
    for i in range(lengths.shape[1]):
        end = end + lengths[0, i]
        start = jnp.maximum(start, jnp.where(end <= pos, end, 0))
    return start


def block_range(info, lengths, rows):
    block = info[0]
    first = lax.div(document_starts(lengths, block * rows), rows)
    last = lax.div(document_starts(lengths, block * rows + rows - 1) + rows - 1, rows)
    n_active = block - first + 1
    return jnp.clip(block - last + 1, 1, n_active), n_active


def attention_steps(info, lengths, q, acc, run_max):
    rows = q.shape[0]
    heads = q.shape[1] // HEAD
    per = heads // KV_HEADS
    factor = math.log2(math.e) / math.sqrt(HEAD)
    block = info[0]
    key_iota = lax.broadcasted_iota(jnp.int32, (rows, rows), 0)
    query_iota = lax.broadcasted_iota(jnp.int32, (rows, rows), 1)
    ones = jnp.ones((EXTRA, rows), BF)
    start = document_starts(lengths, block * rows + lax.broadcasted_iota(jnp.int32, (1, rows), 1))

    def step(load, d, first, masked):
        if masked:
            key_pos = key_iota + (block - d) * rows
            seen = (key_pos >= start) & (key_pos <= query_iota + block * rows)
        ks = [load(slice(None), slice(g * HEAD, (g + 1) * HEAD)) for g in range(KV_HEADS)]
        vts = [
            jnp.concatenate([load(slice(g * HEAD, (g + 1) * HEAD), slice(KV_HEADS * HEAD, None)), ones], axis=0)
            for g in range(KV_HEADS)
        ]

        def score(hs):
            return [dot(ks[h // per], q[:, h * HEAD : (h + 1) * HEAD], ((1,), (1,))) for h in hs]

        def weigh(hs, ss):
            if masked:
                ss = [jnp.where(seen, s, masked_value) for s in ss]
            tops = [jnp.max(s, axis=0, keepdims=True) for s in ss]
            scales = None
            if not first:
                olds = [run_max[h] for h in hs]
                tops = [jnp.maximum(a, b) for a, b in zip(olds, tops)]
                scales = [jnp.exp2((a - b) * factor) for a, b in zip(olds, tops)]
            ws = [jnp.exp2((s - t) * factor).astype(BF) for s, t in zip(ss, tops)]
            for h, t in zip(hs, tops):
                run_max[h] = t
            return ws, scales

        def mix(hs, ws, scales):
            parts = [dot(vts[h // per], w) for h, w in zip(hs, ws)]
            for n, h in enumerate(hs):
                acc[h] = parts[n] if first else acc[h] * scales[n] + parts[n]

        sets = [list(range(a, a + TOGETHER)) for a in range(0, heads, TOGETHER)]
        ss = score(sets[0])
        waiting = None
        for n, hs in enumerate(sets):
            following = score(sets[n + 1]) if n + 1 < len(sets) else None
            weighed = weigh(hs, ss)
            if waiting is not None:
                mix(*waiting)
            waiting = (hs, *weighed)
            ss = following
        mix(*waiting)

    return step


def walk(info, lengths, step, recv, layer, rows):
    low, high = layer * Y_SIZE + 1, (layer + 1) * Y_SIZE

    def other(d, masked):
        src = lax.rem(info[0] - d + 4 * Y_SIZE, Y_SIZE)
        step(lambda a, b: recv[src, layer, a, b], d, False, masked)

    def full(d, c):
        other(d, False)
        return c

    def part(d, c):
        other(d, True)
        return c

    n_full, n_active = block_range(info, lengths, rows)
    n_full = jnp.clip(n_full, low, high)
    lax.fori_loop(low, n_full, full, 0)
    lax.fori_loop(n_full, jnp.clip(n_active, low, high), part, 0)


def near_body(info, lengths, q_far, own, one_up, two_up, acc, run_max, q, sem):
    fetch = pltpu.make_async_copy(q_far, q, sem)
    fetch.start()
    fetch.wait()
    step = attention_steps(info, lengths, q, acc, run_max)
    step(lambda a, b: own[a, b], 0, True, True)
    _, n_active = block_range(info, lengths, q.shape[0])
    for d, ref in ((Y_SIZE, one_up), (2 * Y_SIZE, two_up)):

        @pl.when(d < n_active)
        def _():
            step(lambda a, b: ref[a, b], d, False, True)


def mid_body(info, lengths, q_far, recv, acc, run_max, q, sem):
    fetch = pltpu.make_async_copy(q_far, q, sem)
    fetch.start()
    acc[...] = jnp.zeros_like(acc)
    run_max[...] = jnp.full_like(run_max, masked_value)
    fetch.wait()
    step = attention_steps(info, lengths, q, acc, run_max)
    walk(info, lengths, step, recv, 0, q.shape[0])


def far_body(info, lengths, q_far, recv, acc_a, max_a, acc_b, max_b, out, q, acc, run_max, kept_a, kept_b, straight, sems):
    heads = q.shape[1] // HEAD
    factor = math.log2(math.e) / math.sqrt(HEAD)
    fetch = pltpu.make_async_copy(q_far, q, sems.at[0])
    fetch.start()
    states = (
        pltpu.make_async_copy(acc_a, kept_a, sems.at[1]),
        pltpu.make_async_copy(acc_b, kept_b, sems.at[2]),
    )
    for state in states:
        state.start()
    acc[...] = jnp.zeros_like(acc)
    run_max[...] = jnp.full_like(run_max, masked_value)
    fetch.wait()
    step = attention_steps(info, lengths, q, acc, run_max)
    walk(info, lengths, step, recv, 1, q.shape[0])
    for state in states:
        state.wait()
    for h in range(heads):
        top = jnp.maximum(jnp.maximum(max_a[h], max_b[h]), run_max[h])
        merged = (
            acc[h] * jnp.exp2((run_max[h] - top) * factor)
            + kept_a[h] * jnp.exp2((max_a[h] - top) * factor)
            + kept_b[h] * jnp.exp2((max_b[h] - top) * factor)
        )
        straight[:, h * HEAD : (h + 1) * HEAD] = (merged[:HEAD] / merged[HEAD : HEAD + 1]).T.astype(BF)
    group = out.shape[1] // Z_SIZE
    for y in range(Y_SIZE):

        @pl.when(lax.rem(info[0], Y_SIZE) == y)
        def _():
            cut = y * (group // Y_SIZE)
            for a in range(0, out.shape[1], group):
                both = straight[:, a : a + group]
                if cut:
                    both = jnp.concatenate([both[:, cut:], both[:, :cut]], axis=1)
                out[:, a : a + group] = both


def project_body(info, attn, *refs):
    n = len(PIECES)
    tokens, gain, chosen, residual = refs[2 * n : 2 * n + 4]
    outgoing = refs[2 * n + 4 :]
    z = lax.div(info[0], Y_SIZE)
    part = info[1]
    own = lax.rem(part, 2)
    halves = ((own, refs[:n]), (1 - own, refs[n : 2 * n]))
    rows, width = attn.shape
    unit = width // (Z_SIZE * Y_SIZE)
    cols = width // 2
    tile = 256
    n_experts = len(outgoing)
    cap = outgoing[0].shape[0]
    ids = chosen[...]
    onehot = (lax.broadcasted_iota(jnp.int32, (n_experts, rows), 0) == ids).astype(F32)
    earlier = lax.broadcasted_iota(jnp.int32, (rows, rows), 0) < lax.broadcasted_iota(jnp.int32, (rows, rows), 1)
    before = dot(onehot.astype(BF), earlier.astype(BF))
    slot = jnp.sum(before * onehot, axis=0, keepdims=True).astype(jnp.int32)
    target = (ids ^ part) * cap + slot
    pick = (lax.broadcasted_iota(jnp.int32, (n_experts * cap, rows), 0) == target).astype(BF)
    square = jnp.zeros((rows, 1), F32)
    for half, pieces in halves:
        for j in range(cols // tile):
            here = pl.ds(pl.multiple_of(half * cols + j * tile, tile), tile)
            x = tokens[:, here].astype(F32)
            for piece, (dz, ys) in zip(pieces, PIECES):
                z_at = lax.rem(z - dz + 2 * Z_SIZE, Z_SIZE)
                depth = unit * len(ys)
                rest = pl.ds(pl.multiple_of(z_at * unit * Y_SIZE + unit * ys[0], 2 * unit), depth)
                x = x + dot(attn[:, rest], piece[:, :, j * tile : (j + 1) * tile].reshape(depth, tile))
            x = x.astype(BF)
            residual[:, here] = x
            x = x.astype(F32)
            square = square + jnp.sum(x * x, axis=-1, keepdims=True)
    factor = lax.rsqrt(square / width + norm_epsilon)
    for j in range(width // tile):
        here = slice(j * tile, (j + 1) * tile)
        normed = (residual[:, here].astype(F32) * factor * gain[:, here]).astype(BF)
        sent = dot(pick, normed).astype(BF)
        for s, ref in enumerate(outgoing):
            ref[:, here] = sent[s * cap : (s + 1) * cap]


def expert_body(count, *refs):
    xs, (w_gate, w_up, w_down) = refs[:count], refs[count : count + 3]
    outs = refs[count + 3 : 2 * count + 3]
    x, gates, ups, down, hidden, sems = refs[2 * count + 3 :]
    cap = xs[0].shape[0]
    tiles, _, tile = gates.shape
    copies = []
    for t in range(tiles):
        here = pl.ds(t * tile, tile)
        pair = (
            pltpu.make_async_copy(w_gate.at[:, here], gates.at[t], sems.at[2 * t]),
            pltpu.make_async_copy(w_up.at[:, here], ups.at[t], sems.at[2 * t + 1]),
        )
        for c in pair:
            c.start()
        copies.append(pair)
    last = pltpu.make_async_copy(w_down, down, sems.at[2 * tiles])
    last.start()
    for i, ref in enumerate(xs):
        x[i * cap : (i + 1) * cap, :] = ref[...]
    for t in range(tiles):
        for c in copies[t]:
            c.wait()
        gate = dot(x[...], gates[t])
        up = dot(x[...], ups[t])
        hidden[:, t * tile : (t + 1) * tile] = (gate / (1.0 + jnp.exp(-gate)) * up).astype(BF)
    last.wait()
    wide = 2 * tile
    for j in range(down.shape[1] // wide):
        here = slice(j * wide, (j + 1) * wide)
        out = dot(hidden[...], down[:, here]).astype(BF)
        for i, ref in enumerate(outs):
            ref[:, here] = out[i * cap : (i + 1) * cap]


def combine_body(info, *refs):
    returned = refs[:-4]
    residual, gate_prob, chosen, out = refs[-4:]
    rows = residual.shape[0]
    cap = returned[0].shape[0]
    n_experts = len(returned)
    ids = chosen[...]
    onehot = (lax.broadcasted_iota(jnp.int32, (rows, n_experts), 1) == ids).astype(F32)
    earlier = lax.broadcasted_iota(jnp.int32, (rows, rows), 1) < lax.broadcasted_iota(jnp.int32, (rows, rows), 0)
    before = dot(earlier.astype(BF), onehot.astype(BF))
    slot = jnp.sum(before * onehot, axis=1, keepdims=True).astype(jnp.int32)
    target = (ids ^ info[1]) * cap + slot
    back = None
    for s in range(0, n_experts, 4):
        four = jnp.concatenate([r[...] for r in returned[s : s + 4]], axis=0)
        pick = (lax.broadcasted_iota(jnp.int32, (rows, 4 * cap), 1) + s * cap == target).astype(BF)
        part = dot(pick, four)
        back = part if back is None else back + part
    out[...] = (residual[...].astype(F32) + gate_prob[...] * back).astype(BF)


def on_device(
    tokens,
    queries,
    keys,
    values,
    lengths,
    out_proj,
    norm_gain,
    expert_ids,
    gate_prob,
    w_gate,
    w_up,
    w_down,
):
    rows = tokens.shape[1]
    width = tokens.shape[2]
    heads = queries.shape[2] // HEAD
    n_ctx = lax.axis_size("ctx")
    n_ep = lax.axis_size("ep")
    me = lax.axis_index("ctx")
    y, z = lax.rem(me, Y_SIZE), lax.div(me, Y_SIZE)
    part = lax.axis_index("ep")
    y_groups = [[a * Y_SIZE + b for b in range(Y_SIZE)] for a in range(n_ctx // Y_SIZE)]

    def y_shift(array, by):
        return lax.ppermute(
            array, "ctx", [(a * Y_SIZE + b, a * Y_SIZE + (b + by) % Y_SIZE) for a in range(Z_SIZE) for b in range(Y_SIZE)]
        )

    def z_shift(array, by):
        return lax.ppermute(array, "ctx", [(i, (i + by * Y_SIZE) % n_ctx) for i in range(n_ctx)])

    def core_swap(array):
        return lax.ppermute(array, "ep", [(i, i ^ 1) for i in range(n_ep)])

    pair = jnp.concatenate([keys[0], values[0].T], axis=1)
    half = width // 2
    out_proj, pair = lax.optimization_barrier((out_proj, pair))
    mine = lax.dynamic_slice_in_dim(out_proj, lax.rem(part, 2) * half, half, 1)
    row = jnp.stack([mine] + [y_shift(mine, -s) for s in range(1, Y_SIZE)])
    up, down = [row], [row]
    for _ in range(2):
        up.append(z_shift(up[-1], 1))
        down.append(z_shift(down[-1], -1))

    one_up = z_shift(pair, 1)
    to_after = jnp.arange(Y_SIZE, dtype=jnp.int32)[:, None, None] > y
    two_up = z_shift(one_up, 1)
    to_after = to_after[:, None]
    payload = jnp.where(to_after, jnp.stack([pair, one_up])[None], jnp.stack([one_up, two_up])[None])
    recv = lax.all_to_all(payload, "ctx", 0, 0, axis_index_groups=y_groups)

    info = jnp.stack([me, part]).astype(jnp.int32)
    smem = pl.BlockSpec(memory_space=pltpu.SMEM)
    vmem = pl.BlockSpec(memory_space=pltpu.VMEM)
    anywhere = pl.BlockSpec(memory_space=pl.ANY)
    state = (
        jax.ShapeDtypeStruct((heads, HEAD + EXTRA, rows), F32),
        jax.ShapeDtypeStruct((heads, 1, rows), F32),
    )
    q_room = pltpu.VMEM((rows, width), BF)
    acc_room, max_room = [pltpu.VMEM(s.shape, s.dtype) for s in state]
    acc_a, max_a = call(
        near_body,
        state,
        "near",
        14,
        in_specs=[smem, smem, anywhere] + [vmem] * 3,
        out_specs=(vmem, vmem),
        scratch_shapes=[q_room, pltpu.SemaphoreType.DMA],
        cost_estimate=cost(6e9, 6e6),
    )(info, lengths, queries[0], pair, one_up, two_up)
    acc_b, max_b = call(
        mid_body,
        state,
        "mid",
        14,
        in_specs=[smem, smem, anywhere, vmem],
        out_specs=(vmem, vmem),
        scratch_shapes=[q_room, pltpu.SemaphoreType.DMA],
        cost_estimate=cost(6e9, 6e6),
    )(info, lengths, queries[0], recv)
    held_up, held_down, max_a = lax.optimization_barrier((up[-1], down[-1], max_a))
    up.append(z_shift(held_up, 1))
    down.append(z_shift(held_down, -1))
    held_up, held_down, max_b = lax.optimization_barrier((up[-1][: Y_SIZE // 2], down[-1][Y_SIZE // 2 :], max_b))
    last_up = z_shift(held_up, 1)
    last_down = z_shift(held_down, -1)
    own_pieces = up + down[1:]
    other_pieces = [core_swap(piece) for piece in own_pieces]
    attn = call(
        far_body,
        jax.ShapeDtypeStruct((rows, width), BF),
        "far",
        20,
        in_specs=[smem, smem, anywhere, vmem, anywhere, vmem, anywhere, vmem],
        out_specs=vmem,
        scratch_shapes=[q_room, acc_room, max_room, acc_room, acc_room, q_room, pltpu.SemaphoreType.DMA((3,))],
        cost_estimate=cost(8e9, 8e6),
    )(info, lengths, queries[0], recv, acc_a, max_a, acc_b, max_b)

    own_pieces += [last_up, last_down]
    other_pieces += [core_swap(last_up), core_swap(last_down)]

    chunk = jax.ShapeDtypeStruct((CAP, width), BF)
    n_pieces = len(own_pieces)
    residual, *outgoing = call(
        project_body,
        (jax.ShapeDtypeStruct((rows, width), BF),) + (chunk,) * n_ep,
        "project",
        14,
        in_specs=[smem] + [vmem] * (2 * n_pieces + 4),
        out_specs=(vmem,) * (1 + n_ep),
        cost_estimate=cost(2.6e9, 1.4e7),
    )(info, attn, *own_pieces, *other_pieces, tokens[0], norm_gain[None, :], expert_ids[:, :, 0])

    def partner(array, s):
        return lax.ppermute(array, "ep", [(i, i ^ s) for i in range(n_ep)])

    tile = 256
    ffe = w_gate.shape[2]

    def experts(members, name):
        n = len(members)
        outs = call(
            lambda *refs: expert_body(n, *refs),
            (chunk,) * n,
            name,
            24,
            in_specs=[vmem] * n + [anywhere] * 3,
            out_specs=(vmem,) * n,
            scratch_shapes=[
                pltpu.VMEM((n * CAP, width), BF),
                pltpu.VMEM((ffe // tile, width, tile), BF),
                pltpu.VMEM((ffe // tile, width, tile), BF),
                pltpu.VMEM((ffe, width), BF),
                pltpu.VMEM((n * CAP, ffe), BF),
                pltpu.SemaphoreType.DMA((2 * (ffe // tile) + 1,)),
            ],
            cost_estimate=cost(n * CAP * 6 * width * ffe, 1e7),
        )(*[incoming[s] for s in members], w_gate[0], w_up[0], w_down[0])
        answers.update(zip(members, outs))

    answers = {}
    incoming = {s: partner(outgoing[s], s) for s in (4, 5, 2, 3, 6, 7, 1)}
    incoming[0] = outgoing[0]
    experts((0, 1), "experts_self")
    incoming[4], answers[0] = lax.optimization_barrier((incoming[4], answers[0]))
    experts((4, 5), "experts_far")
    experts((2, 3, 6, 7), "experts_near")
    returned = [answers[0] if s == 0 else partner(answers[s], s) for s in range(n_ep)]

    layer_out = call(
        combine_body,
        jax.ShapeDtypeStruct((rows, width), BF),
        "combine",
        14,
        in_specs=[smem] + [vmem] * (n_ep + 3),
        out_specs=vmem,
    )(info, *returned, residual, gate_prob[0], expert_ids[0])
    return layer_out[None]


def solution(mesh):
    placed = (
        P("ep", "ctx", None),
        P("ep", "ctx", None),
        P("ep", "ctx", None),
        P("ep", "ctx", None),
        P("ep", None),
        P("ctx", None),
        P(),
        P("ep", "ctx", None),
        P("ep", "ctx", None),
        P("ep", None, None),
        P("ep", None, None),
        P("ep", None, None),
    )
    return jax.shard_map(
        on_device, mesh=mesh, in_specs=placed, out_specs=P("ep", "ctx", None), check_vma=False
    )
```

```python
import math

import jax
import jax.numpy as jnp
from jax import lax
from jax.experimental import pallas as pl
from jax.experimental.pallas import tpu as pltpu
from jax.sharding import PartitionSpec as P

HEAD = 128
CAP = 64
KV_HEADS = 2
Y_SIZE = 4
Z_SIZE = 8
ALL_Y = (0, 1, 2, 3)
PIECES = tuple((dz, ALL_Y) for dz in (0, 1, 2, 3, -1, -2, -3, 4))
EXTRA = 16
TOGETHER = 4

masked_value = -1e30
norm_epsilon = 1e-06
BF = jnp.bfloat16
F32 = jnp.float32


def call(body, out_shape, name, vmem_mb=48, **kw):
    return pl.pallas_call(
        body,
        out_shape=out_shape,
        name=name,
        compiler_params=pltpu.CompilerParams(vmem_limit_bytes=vmem_mb * 1024 * 1024),
        **kw,
    )


def cost(flops, size):
    return pl.CostEstimate(flops=int(flops), bytes_accessed=int(size), transcendentals=0)


def dot(a, b, dims=((1,), (0,))):
    return lax.dot_general(a, b, (dims, ((), ())), preferred_element_type=F32)


def document_starts(lengths, pos):
    end, start = 0, jnp.zeros_like(pos)
    for i in range(lengths.shape[1]):
        end = end + lengths[0, i]
        start = jnp.maximum(start, jnp.where(end <= pos, end, 0))
    return start


def block_range(info, lengths, rows):
    block = info[0]
    first = lax.div(document_starts(lengths, block * rows), rows)
    last = lax.div(document_starts(lengths, block * rows + rows - 1) + rows - 1, rows)
    n_active = block - first + 1
    return jnp.clip(block - last + 1, 1, n_active), n_active


def attention_steps(info, lengths, q, acc, run_max):
    rows = q.shape[0]
    heads = q.shape[1] // HEAD
    per = heads // KV_HEADS
    factor = math.log2(math.e) / math.sqrt(HEAD)
    block = info[0]
    key_iota = lax.broadcasted_iota(jnp.int32, (rows, rows), 0)
    query_iota = lax.broadcasted_iota(jnp.int32, (rows, rows), 1)
    ones = jnp.ones((EXTRA, rows), BF)
    start = document_starts(lengths, block * rows + lax.broadcasted_iota(jnp.int32, (1, rows), 1))

    def step(load, d, first, masked):
        if masked:
            key_pos = key_iota + (block - d) * rows
            seen = (key_pos >= start) & (key_pos <= query_iota + block * rows)
        ks = [load(slice(None), slice(g * HEAD, (g + 1) * HEAD)) for g in range(KV_HEADS)]
        vts = [
            jnp.concatenate([load(slice(g * HEAD, (g + 1) * HEAD), slice(KV_HEADS * HEAD, None)), ones], axis=0)
            for g in range(KV_HEADS)
        ]

        def score(hs):
            return [dot(ks[h // per], q[:, h * HEAD : (h + 1) * HEAD], ((1,), (1,))) for h in hs]

        def weigh(hs, ss):
            if masked:
                ss = [jnp.where(seen, s, masked_value) for s in ss]
            tops = [jnp.max(s, axis=0, keepdims=True) for s in ss]
            scales = None
            if not first:
                olds = [run_max[h] for h in hs]
                tops = [jnp.maximum(a, b) for a, b in zip(olds, tops)]
                scales = [jnp.exp2((a - b) * factor) for a, b in zip(olds, tops)]
            ws = [jnp.exp2((s - t) * factor).astype(BF) for s, t in zip(ss, tops)]
            for h, t in zip(hs, tops):
                run_max[h] = t
            return ws, scales

        def mix(hs, ws, scales):
            parts = [dot(vts[h // per], w) for h, w in zip(hs, ws)]
            for n, h in enumerate(hs):
                acc[h] = parts[n] if first else acc[h] * scales[n] + parts[n]

        sets = [list(range(a, a + TOGETHER)) for a in range(0, heads, TOGETHER)]
        ss = score(sets[0])
        waiting = None
        for n, hs in enumerate(sets):
            following = score(sets[n + 1]) if n + 1 < len(sets) else None
            weighed = weigh(hs, ss)
            if waiting is not None:
                mix(*waiting)
            waiting = (hs, *weighed)
            ss = following
        mix(*waiting)

    return step


def walk(info, lengths, step, recv, layer, rows):
    low, high = layer * Y_SIZE + 1, (layer + 1) * Y_SIZE

    def other(d, masked):
        src = lax.rem(info[0] - d + 4 * Y_SIZE, Y_SIZE)
        step(lambda a, b: recv[src, layer, a, b], d, False, masked)

    def full(d, c):
        other(d, False)
        return c

    def part(d, c):
        other(d, True)
        return c

    n_full, n_active = block_range(info, lengths, rows)
    n_full = jnp.clip(n_full, low, high)
    lax.fori_loop(low, n_full, full, 0)
    lax.fori_loop(n_full, jnp.clip(n_active, low, high), part, 0)


def near_body(info, lengths, q_far, own, one_up, two_up, acc, run_max, q, sem):
    fetch = pltpu.make_async_copy(q_far, q, sem)
    fetch.start()
    fetch.wait()
    step = attention_steps(info, lengths, q, acc, run_max)
    step(lambda a, b: own[a, b], 0, True, True)
    _, n_active = block_range(info, lengths, q.shape[0])
    for d, ref in ((Y_SIZE, one_up), (2 * Y_SIZE, two_up)):

        @pl.when(d < n_active)
        def _():
            step(lambda a, b: ref[a, b], d, False, True)


def mid_body(info, lengths, q_far, recv, acc, run_max, q, sem):
    fetch = pltpu.make_async_copy(q_far, q, sem)
    fetch.start()
    acc[...] = jnp.zeros_like(acc)
    run_max[...] = jnp.full_like(run_max, masked_value)
    fetch.wait()
    step = attention_steps(info, lengths, q, acc, run_max)
    walk(info, lengths, step, recv, 0, q.shape[0])


def far_body(info, lengths, q_far, recv, acc_a, max_a, acc_b, max_b, out, q, acc, run_max, kept_a, kept_b, straight, sems):
    heads = q.shape[1] // HEAD
    factor = math.log2(math.e) / math.sqrt(HEAD)
    fetch = pltpu.make_async_copy(q_far, q, sems.at[0])
    fetch.start()
    states = (
        pltpu.make_async_copy(acc_a, kept_a, sems.at[1]),
        pltpu.make_async_copy(acc_b, kept_b, sems.at[2]),
    )
    for state in states:
        state.start()
    acc[...] = jnp.zeros_like(acc)
    run_max[...] = jnp.full_like(run_max, masked_value)
    fetch.wait()
    step = attention_steps(info, lengths, q, acc, run_max)
    walk(info, lengths, step, recv, 1, q.shape[0])
    for state in states:
        state.wait()
    for h in range(heads):
        top = jnp.maximum(jnp.maximum(max_a[h], max_b[h]), run_max[h])
        merged = (
            acc[h] * jnp.exp2((run_max[h] - top) * factor)
            + kept_a[h] * jnp.exp2((max_a[h] - top) * factor)
            + kept_b[h] * jnp.exp2((max_b[h] - top) * factor)
        )
        straight[:, h * HEAD : (h + 1) * HEAD] = (merged[:HEAD] / merged[HEAD : HEAD + 1]).T.astype(BF)
    group = out.shape[1] // Z_SIZE
    for y in range(Y_SIZE):

        @pl.when(lax.rem(info[0], Y_SIZE) == y)
        def _():
            cut = y * (group // Y_SIZE)
            for a in range(0, out.shape[1], group):
                both = straight[:, a : a + group]
                if cut:
                    both = jnp.concatenate([both[:, cut:], both[:, :cut]], axis=1)
                out[:, a : a + group] = both


def project_body(info, attn, *refs):
    n = len(PIECES)
    tokens, gain, chosen, residual = refs[2 * n : 2 * n + 4]
    outgoing = refs[2 * n + 4 :]
    z = lax.div(info[0], Y_SIZE)
    part = info[1]
    own = lax.rem(part, 2)
    halves = ((own, refs[:n]), (1 - own, refs[n : 2 * n]))
    rows, width = attn.shape
    unit = width // (Z_SIZE * Y_SIZE)
    cols = width // 2
    tile = 256
    n_experts = len(outgoing)
    cap = outgoing[0].shape[0]
    ids = chosen[...]
    onehot = (lax.broadcasted_iota(jnp.int32, (n_experts, rows), 0) == ids).astype(F32)
    earlier = lax.broadcasted_iota(jnp.int32, (rows, rows), 0) < lax.broadcasted_iota(jnp.int32, (rows, rows), 1)
    before = dot(onehot.astype(BF), earlier.astype(BF))
    slot = jnp.sum(before * onehot, axis=0, keepdims=True).astype(jnp.int32)
    target = (ids ^ part) * cap + slot
    pick = (lax.broadcasted_iota(jnp.int32, (n_experts * cap, rows), 0) == target).astype(BF)
    square = jnp.zeros((rows, 1), F32)
    for half, pieces in halves:
        for j in range(cols // tile):
            here = pl.ds(pl.multiple_of(half * cols + j * tile, tile), tile)
            x = tokens[:, here].astype(F32)
            for piece, (dz, ys) in zip(pieces, PIECES):
                z_at = lax.rem(z - dz + 2 * Z_SIZE, Z_SIZE)
                depth = unit * len(ys)
                rest = pl.ds(pl.multiple_of(z_at * unit * Y_SIZE + unit * ys[0], 2 * unit), depth)
                x = x + dot(attn[:, rest], piece[:, :, j * tile : (j + 1) * tile].reshape(depth, tile))
            x = x.astype(BF)
            residual[:, here] = x
            x = x.astype(F32)
            square = square + jnp.sum(x * x, axis=-1, keepdims=True)
    factor = lax.rsqrt(square / width + norm_epsilon)
    for j in range(width // tile):
        here = slice(j * tile, (j + 1) * tile)
        normed = (residual[:, here].astype(F32) * factor * gain[:, here]).astype(BF)
        sent = dot(pick, normed).astype(BF)
        for s, ref in enumerate(outgoing):
            ref[:, here] = sent[s * cap : (s + 1) * cap]


def expert_body(count, *refs):
    xs, (w_gate, w_up, w_down) = refs[:count], refs[count : count + 3]
    outs = refs[count + 3 : 2 * count + 3]
    x, gates, ups, down, hidden, sems = refs[2 * count + 3 :]
    cap = xs[0].shape[0]
    tiles, _, tile = gates.shape
    copies = []
    for t in range(tiles):
        here = pl.ds(t * tile, tile)
        pair = (
            pltpu.make_async_copy(w_gate.at[:, here], gates.at[t], sems.at[2 * t]),
            pltpu.make_async_copy(w_up.at[:, here], ups.at[t], sems.at[2 * t + 1]),
        )
        for c in pair:
            c.start()
        copies.append(pair)
    last = pltpu.make_async_copy(w_down, down, sems.at[2 * tiles])
    last.start()
    for i, ref in enumerate(xs):
        x[i * cap : (i + 1) * cap, :] = ref[...]
    for t in range(tiles):
        for c in copies[t]:
            c.wait()
        gate = dot(x[...], gates[t])
        up = dot(x[...], ups[t])
        hidden[:, t * tile : (t + 1) * tile] = (gate / (1.0 + jnp.exp(-gate)) * up).astype(BF)
    last.wait()
    wide = 2 * tile
    for j in range(down.shape[1] // wide):
        here = slice(j * wide, (j + 1) * wide)
        out = dot(hidden[...], down[:, here]).astype(BF)
        for i, ref in enumerate(outs):
            ref[:, here] = out[i * cap : (i + 1) * cap]


def combine_body(info, *refs):
    returned = refs[:-4]
    residual, gate_prob, chosen, out = refs[-4:]
    rows = residual.shape[0]
    cap = returned[0].shape[0]
    n_experts = len(returned)
    ids = chosen[...]
    onehot = (lax.broadcasted_iota(jnp.int32, (rows, n_experts), 1) == ids).astype(F32)
    earlier = lax.broadcasted_iota(jnp.int32, (rows, rows), 1) < lax.broadcasted_iota(jnp.int32, (rows, rows), 0)
    before = dot(earlier.astype(BF), onehot.astype(BF))
    slot = jnp.sum(before * onehot, axis=1, keepdims=True).astype(jnp.int32)
    target = (ids ^ info[1]) * cap + slot
    back = None
    for s in range(0, n_experts, 4):
        four = jnp.concatenate([r[...] for r in returned[s : s + 4]], axis=0)
        pick = (lax.broadcasted_iota(jnp.int32, (rows, 4 * cap), 1) + s * cap == target).astype(BF)
        part = dot(pick, four)
        back = part if back is None else back + part
    out[...] = (residual[...].astype(F32) + gate_prob[...] * back).astype(BF)


def on_device(
    tokens,
    queries,
    keys,
    values,
    lengths,
    out_proj,
    norm_gain,
    expert_ids,
    gate_prob,
    w_gate,
    w_up,
    w_down,
):
    rows = tokens.shape[1]
    width = tokens.shape[2]
    heads = queries.shape[2] // HEAD
    n_ctx = lax.axis_size("ctx")
    n_ep = lax.axis_size("ep")
    me = lax.axis_index("ctx")
    y, z = lax.rem(me, Y_SIZE), lax.div(me, Y_SIZE)
    part = lax.axis_index("ep")
    y_groups = [[a * Y_SIZE + b for b in range(Y_SIZE)] for a in range(n_ctx // Y_SIZE)]

    def y_shift(array, by):
        return lax.ppermute(
            array, "ctx", [(a * Y_SIZE + b, a * Y_SIZE + (b + by) % Y_SIZE) for a in range(Z_SIZE) for b in range(Y_SIZE)]
        )

    def z_shift(array, by):
        return lax.ppermute(array, "ctx", [(i, (i + by * Y_SIZE) % n_ctx) for i in range(n_ctx)])

    def core_swap(array):
        return lax.ppermute(array, "ep", [(i, i ^ 1) for i in range(n_ep)])

    pair = jnp.concatenate([keys[0], values[0].T], axis=1)
    half = width // 2
    out_proj, pair = lax.optimization_barrier((out_proj, pair))
    mine = lax.dynamic_slice_in_dim(out_proj, lax.rem(part, 2) * half, half, 1)
    across = z_shift(mine, Z_SIZE // 2)
    row = jnp.stack([mine] + [y_shift(mine, -s) for s in range(1, Y_SIZE)])
    row, across = lax.optimization_barrier((row, across))
    opposite = jnp.stack([across] + [y_shift(across, -s) for s in range(1, Y_SIZE)])
    up, down = [row], [row]
    for _ in range(2):
        up.append(z_shift(up[-1], 1))
        down.append(z_shift(down[-1], -1))

    one_up = z_shift(pair, 1)
    to_after = jnp.arange(Y_SIZE, dtype=jnp.int32)[:, None, None] > y
    two_up = z_shift(one_up, 1)
    to_after = to_after[:, None]
    payload = jnp.where(to_after, jnp.stack([pair, one_up])[None], jnp.stack([one_up, two_up])[None])
    payload, opposite = lax.optimization_barrier((payload, opposite))
    recv = lax.all_to_all(payload, "ctx", 0, 0, axis_index_groups=y_groups)

    info = jnp.stack([me, part]).astype(jnp.int32)
    smem = pl.BlockSpec(memory_space=pltpu.SMEM)
    vmem = pl.BlockSpec(memory_space=pltpu.VMEM)
    anywhere = pl.BlockSpec(memory_space=pl.ANY)
    state = (
        jax.ShapeDtypeStruct((heads, HEAD + EXTRA, rows), F32),
        jax.ShapeDtypeStruct((heads, 1, rows), F32),
    )
    q_room = pltpu.VMEM((rows, width), BF)
    acc_room, max_room = [pltpu.VMEM(s.shape, s.dtype) for s in state]
    acc_a, max_a = call(
        near_body,
        state,
        "near",
        14,
        in_specs=[smem, smem, anywhere] + [vmem] * 3,
        out_specs=(vmem, vmem),
        scratch_shapes=[q_room, pltpu.SemaphoreType.DMA],
        cost_estimate=cost(6e9, 6e6),
    )(info, lengths, queries[0], pair, one_up, two_up)
    acc_b, max_b = call(
        mid_body,
        state,
        "mid",
        14,
        in_specs=[smem, smem, anywhere, vmem],
        out_specs=(vmem, vmem),
        scratch_shapes=[q_room, pltpu.SemaphoreType.DMA],
        cost_estimate=cost(6e9, 6e6),
    )(info, lengths, queries[0], recv)
    held_up, held_down, max_a = lax.optimization_barrier((up[-1], down[-1], max_a))
    up.append(z_shift(held_up, 1))
    down.append(z_shift(held_down, -1))
    own_pieces = up + down[1:] + [opposite]
    up_2, down_2, swap_4, max_b = lax.optimization_barrier((up[2], down[2], opposite, max_b))
    ready = [up[0], up[1], up_2, up[3], down[1], down_2, down[3], swap_4]
    other_pieces = [core_swap(piece) for piece in ready]
    attn = call(
        far_body,
        jax.ShapeDtypeStruct((rows, width), BF),
        "far",
        20,
        in_specs=[smem, smem, anywhere, vmem, anywhere, vmem, anywhere, vmem],
        out_specs=vmem,
        scratch_shapes=[q_room, acc_room, max_room, acc_room, acc_room, q_room, pltpu.SemaphoreType.DMA((3,))],
        cost_estimate=cost(8e9, 8e6),
    )(info, lengths, queries[0], recv, acc_a, max_a, acc_b, max_b)


    chunk = jax.ShapeDtypeStruct((CAP, width), BF)
    n_pieces = len(own_pieces)
    residual, *outgoing = call(
        project_body,
        (jax.ShapeDtypeStruct((rows, width), BF),) + (chunk,) * n_ep,
        "project",
        14,
        in_specs=[smem] + [vmem] * (2 * n_pieces + 4),
        out_specs=(vmem,) * (1 + n_ep),
        cost_estimate=cost(2.6e9, 1.4e7),
    )(info, attn, *own_pieces, *other_pieces, tokens[0], norm_gain[None, :], expert_ids[:, :, 0])

    def partner(array, s):
        return lax.ppermute(array, "ep", [(i, i ^ s) for i in range(n_ep)])

    tile = 256
    ffe = w_gate.shape[2]

    def experts(members, name):
        n = len(members)
        outs = call(
            lambda *refs: expert_body(n, *refs),
            (chunk,) * n,
            name,
            24,
            in_specs=[vmem] * n + [anywhere] * 3,
            out_specs=(vmem,) * n,
            scratch_shapes=[
                pltpu.VMEM((n * CAP, width), BF),
                pltpu.VMEM((ffe // tile, width, tile), BF),
                pltpu.VMEM((ffe // tile, width, tile), BF),
                pltpu.VMEM((ffe, width), BF),
                pltpu.VMEM((n * CAP, ffe), BF),
                pltpu.SemaphoreType.DMA((2 * (ffe // tile) + 1,)),
            ],
            cost_estimate=cost(n * CAP * 6 * width * ffe, 1e7),
        )(*[incoming[s] for s in members], w_gate[0], w_up[0], w_down[0])
        answers.update(zip(members, outs))

    answers = {}
    incoming = {s: partner(outgoing[s], s) for s in (4, 5, 2, 3, 6, 7, 1)}
    incoming[0] = outgoing[0]
    experts((0, 1), "experts_self")
    incoming[4], answers[0] = lax.optimization_barrier((incoming[4], answers[0]))
    experts((4, 5), "experts_far")
    experts((2, 3, 6, 7), "experts_near")
    returned = [answers[0] if s == 0 else partner(answers[s], s) for s in range(n_ep)]

    layer_out = call(
        combine_body,
        jax.ShapeDtypeStruct((rows, width), BF),
        "combine",
        14,
        in_specs=[smem] + [vmem] * (n_ep + 3),
        out_specs=vmem,
    )(info, *returned, residual, gate_prob[0], expert_ids[0])
    return layer_out[None]


def solution(mesh):
    placed = (
        P("ep", "ctx", None),
        P("ep", "ctx", None),
        P("ep", "ctx", None),
        P("ep", "ctx", None),
        P("ep", None),
        P("ctx", None),
        P(),
        P("ep", "ctx", None),
        P("ep", "ctx", None),
        P("ep", None, None),
        P("ep", None, None),
        P("ep", None, None),
    )
    return jax.shard_map(
        on_device, mesh=mesh, in_specs=placed, out_specs=P("ep", "ctx", None), check_vma=False
    )
```

```python
import math

import jax
import jax.numpy as jnp
from jax import lax
from jax.experimental import pallas as pl
from jax.experimental.pallas import tpu as pltpu
from jax.sharding import PartitionSpec as P

HEAD = 128
CAP = 64
KV_HEADS = 2
Y_SIZE = 4
Z_SIZE = 8
ALL_Y = (0, 1, 2, 3)
PIECES = tuple((dz, ALL_Y) for dz in (0, 1, 2, 3, -1, -2, -3, 4))
EXTRA = 16
TOGETHER = 4

masked_value = -1e30
norm_epsilon = 1e-06
BF = jnp.bfloat16
F32 = jnp.float32


def call(body, out_shape, name, vmem_mb=48, **kw):
    return pl.pallas_call(
        body,
        out_shape=out_shape,
        name=name,
        compiler_params=pltpu.CompilerParams(vmem_limit_bytes=vmem_mb * 1024 * 1024),
        **kw,
    )


def cost(flops, size):
    return pl.CostEstimate(flops=int(flops), bytes_accessed=int(size), transcendentals=0)


def dot(a, b, dims=((1,), (0,))):
    return lax.dot_general(a, b, (dims, ((), ())), preferred_element_type=F32)


def document_starts(lengths, pos):
    end, start = 0, jnp.zeros_like(pos)
    for i in range(lengths.shape[1]):
        end = end + lengths[0, i]
        start = jnp.maximum(start, jnp.where(end <= pos, end, 0))
    return start


def block_range(info, lengths, rows):
    block = info[0]
    first = lax.div(document_starts(lengths, block * rows), rows)
    last = lax.div(document_starts(lengths, block * rows + rows - 1) + rows - 1, rows)
    n_active = block - first + 1
    return jnp.clip(block - last + 1, 1, n_active), n_active


def attention_steps(info, lengths, q, acc, run_max):
    rows = q.shape[0]
    heads = q.shape[1] // HEAD
    per = heads // KV_HEADS
    factor = math.log2(math.e) / math.sqrt(HEAD)
    block = info[0]
    key_iota = lax.broadcasted_iota(jnp.int32, (rows, rows), 0)
    query_iota = lax.broadcasted_iota(jnp.int32, (rows, rows), 1)
    ones = jnp.ones((EXTRA, rows), BF)
    start = document_starts(lengths, block * rows + lax.broadcasted_iota(jnp.int32, (1, rows), 1))

    def step(load, d, first, masked):
        if masked:
            key_pos = key_iota + (block - d) * rows
            seen = (key_pos >= start) & (key_pos <= query_iota + block * rows)
        ks = [load(slice(None), slice(g * HEAD, (g + 1) * HEAD)) for g in range(KV_HEADS)]
        vts = [
            jnp.concatenate([load(slice(g * HEAD, (g + 1) * HEAD), slice(KV_HEADS * HEAD, None)), ones], axis=0)
            for g in range(KV_HEADS)
        ]

        def score(hs):
            return [dot(ks[h // per], q[:, h * HEAD : (h + 1) * HEAD], ((1,), (1,))) for h in hs]

        def weigh(hs, ss):
            if masked:
                ss = [jnp.where(seen, s, masked_value) for s in ss]
            tops = [jnp.max(s, axis=0, keepdims=True) for s in ss]
            scales = None
            if not first:
                olds = [run_max[h] for h in hs]
                tops = [jnp.maximum(a, b) for a, b in zip(olds, tops)]
                scales = [jnp.exp2((a - b) * factor) for a, b in zip(olds, tops)]
            ws = [jnp.exp2((s - t) * factor).astype(BF) for s, t in zip(ss, tops)]
            for h, t in zip(hs, tops):
                run_max[h] = t
            return ws, scales

        def mix(hs, ws, scales):
            parts = [dot(vts[h // per], w) for h, w in zip(hs, ws)]
            for n, h in enumerate(hs):
                acc[h] = parts[n] if first else acc[h] * scales[n] + parts[n]

        sets = [list(range(a, a + TOGETHER)) for a in range(0, heads, TOGETHER)]
        ss = score(sets[0])
        waiting = None
        for n, hs in enumerate(sets):
            following = score(sets[n + 1]) if n + 1 < len(sets) else None
            weighed = weigh(hs, ss)
            if waiting is not None:
                mix(*waiting)
            waiting = (hs, *weighed)
            ss = following
        mix(*waiting)

    return step


def walk(info, lengths, step, recv, layer, rows):
    low, high = layer * Y_SIZE + 1, (layer + 1) * Y_SIZE

    def other(d, masked):
        src = lax.rem(info[0] - d + 4 * Y_SIZE, Y_SIZE)
        step(lambda a, b: recv[src, layer, a, b], d, False, masked)

    def full(d, c):
        other(d, False)
        return c

    def part(d, c):
        other(d, True)
        return c

    n_full, n_active = block_range(info, lengths, rows)
    n_full = jnp.clip(n_full, low, high)
    lax.fori_loop(low, n_full, full, 0)
    lax.fori_loop(n_full, jnp.clip(n_active, low, high), part, 0)


def near_body(info, lengths, q_far, own, payload, acc, run_max, q, ups, sems):
    fetches = (
        pltpu.make_async_copy(q_far, q, sems.at[0]),
        pltpu.make_async_copy(payload.at[0], ups, sems.at[1]),
    )
    for fetch in fetches:
        fetch.start()
    for fetch in fetches:
        fetch.wait()
    step = attention_steps(info, lengths, q, acc, run_max)
    step(lambda a, b: own[a, b], 0, True, True)
    _, n_active = block_range(info, lengths, q.shape[0])
    for i in range(ups.shape[0]):
        d = (i + 1) * Y_SIZE

        @pl.when(d < n_active)
        def _():
            step(lambda a, b: ups[i, a, b], d, False, True)


def mid_body(info, lengths, q_far, recv, acc, run_max, q, sem):
    fetch = pltpu.make_async_copy(q_far, q, sem)
    fetch.start()
    acc[...] = jnp.zeros_like(acc)
    run_max[...] = jnp.full_like(run_max, masked_value)
    fetch.wait()
    step = attention_steps(info, lengths, q, acc, run_max)
    walk(info, lengths, step, recv, 0, q.shape[0])


def far_body(info, lengths, q_far, recv, acc_a, max_a, acc_b, max_b, out, q, acc, run_max, kept_a, kept_b, straight, sems):
    heads = q.shape[1] // HEAD
    factor = math.log2(math.e) / math.sqrt(HEAD)
    fetch = pltpu.make_async_copy(q_far, q, sems.at[0])
    fetch.start()
    states = (
        pltpu.make_async_copy(acc_a, kept_a, sems.at[1]),
        pltpu.make_async_copy(acc_b, kept_b, sems.at[2]),
    )
    for state in states:
        state.start()
    acc[...] = jnp.zeros_like(acc)
    run_max[...] = jnp.full_like(run_max, masked_value)
    fetch.wait()
    step = attention_steps(info, lengths, q, acc, run_max)
    walk(info, lengths, step, recv, 1, q.shape[0])
    for state in states:
        state.wait()
    for h in range(heads):
        top = jnp.maximum(jnp.maximum(max_a[h], max_b[h]), run_max[h])
        merged = (
            acc[h] * jnp.exp2((run_max[h] - top) * factor)
            + kept_a[h] * jnp.exp2((max_a[h] - top) * factor)
            + kept_b[h] * jnp.exp2((max_b[h] - top) * factor)
        )
        straight[:, h * HEAD : (h + 1) * HEAD] = (merged[:HEAD] / merged[HEAD : HEAD + 1]).T.astype(BF)
    group = out.shape[1] // Z_SIZE
    for y in range(Y_SIZE):

        @pl.when(lax.rem(info[0], Y_SIZE) == y)
        def _():
            cut = y * (group // Y_SIZE)
            for a in range(0, out.shape[1], group):
                both = straight[:, a : a + group]
                if cut:
                    both = jnp.concatenate([both[:, cut:], both[:, :cut]], axis=1)
                out[:, a : a + group] = both


def slots_body(n_experts, cap, info, across, down, target_across, target_down):
    rows = down.shape[0]
    first = lax.broadcasted_iota(jnp.int32, (rows, rows), 0)
    second = lax.broadcasted_iota(jnp.int32, (rows, rows), 1)
    ids = across[...]
    onehot = (lax.broadcasted_iota(jnp.int32, (n_experts, rows), 0) == ids).astype(F32)
    before = dot(onehot.astype(BF), (first < second).astype(BF))
    slot = jnp.sum(before * onehot, axis=0, keepdims=True).astype(jnp.int32)
    target_across[...] = (ids ^ info[1]) * cap + slot
    ids = down[...]
    onehot = (lax.broadcasted_iota(jnp.int32, (rows, n_experts), 1) == ids).astype(F32)
    before = dot((second < first).astype(BF), onehot.astype(BF))
    slot = jnp.sum(before * onehot, axis=1, keepdims=True).astype(jnp.int32)
    target_down[...] = (ids ^ info[1]) * cap + slot


def project_body(info, attn, *refs):
    n = len(PIECES)
    tokens, gain, target, residual = refs[2 * n : 2 * n + 4]
    outgoing = refs[2 * n + 4 :]
    z = lax.div(info[0], Y_SIZE)
    part = info[1]
    own = lax.rem(part, 2)
    halves = ((own, refs[:n]), (1 - own, refs[n : 2 * n]))
    rows, width = attn.shape
    unit = width // (Z_SIZE * Y_SIZE)
    cols = width // 2
    tile = 256
    n_experts = len(outgoing)
    cap = outgoing[0].shape[0]
    pick = (lax.broadcasted_iota(jnp.int32, (n_experts * cap, rows), 0) == target[...]).astype(BF)
    square = jnp.zeros((rows, 1), F32)
    for half, pieces in halves:
        for j in range(cols // tile):
            here = pl.ds(pl.multiple_of(half * cols + j * tile, tile), tile)
            x = tokens[:, here].astype(F32)
            for piece, (dz, ys) in zip(pieces, PIECES):
                z_at = lax.rem(z - dz + 2 * Z_SIZE, Z_SIZE)
                depth = unit * len(ys)
                rest = pl.ds(pl.multiple_of(z_at * unit * Y_SIZE + unit * ys[0], 2 * unit), depth)
                x = x + dot(attn[:, rest], piece[:, :, j * tile : (j + 1) * tile].reshape(depth, tile))
            x = x.astype(BF)
            residual[:, here] = x
            x = x.astype(F32)
            square = square + jnp.sum(x * x, axis=-1, keepdims=True)
    factor = lax.rsqrt(square / width + norm_epsilon)
    for j in range(width // tile):
        here = slice(j * tile, (j + 1) * tile)
        normed = (residual[:, here].astype(F32) * factor * gain[:, here]).astype(BF)
        sent = dot(pick, normed).astype(BF)
        for s, ref in enumerate(outgoing):
            ref[:, here] = sent[s * cap : (s + 1) * cap]


def expert_body(count, *refs):
    xs, (w_gate, w_up, w_down) = refs[:count], refs[count : count + 3]
    outs = refs[count + 3 : 2 * count + 3]
    x, gates, ups, down, hidden, sems = refs[2 * count + 3 :]
    cap = xs[0].shape[0]
    tiles, _, tile = gates.shape
    copies = []
    for t in range(tiles):
        here = pl.ds(t * tile, tile)
        pair = (
            pltpu.make_async_copy(w_gate.at[:, here], gates.at[t], sems.at[2 * t]),
            pltpu.make_async_copy(w_up.at[:, here], ups.at[t], sems.at[2 * t + 1]),
        )
        for c in pair:
            c.start()
        copies.append(pair)
    last = pltpu.make_async_copy(w_down, down, sems.at[2 * tiles])
    last.start()
    for i, ref in enumerate(xs):
        x[i * cap : (i + 1) * cap, :] = ref[...]
    for t in range(tiles):
        for c in copies[t]:
            c.wait()
        gate = dot(x[...], gates[t])
        up = dot(x[...], ups[t])
        hidden[:, t * tile : (t + 1) * tile] = (gate / (1.0 + jnp.exp(-gate)) * up).astype(BF)
    last.wait()
    wide = 2 * tile
    for j in range(down.shape[1] // wide):
        here = slice(j * wide, (j + 1) * wide)
        out = dot(hidden[...], down[:, here]).astype(BF)
        for i, ref in enumerate(outs):
            ref[:, here] = out[i * cap : (i + 1) * cap]


def combine_body(*refs):
    returned = refs[:-4]
    residual, gate_prob, target, out = refs[-4:]
    rows = residual.shape[0]
    cap = returned[0].shape[0]
    n_experts = len(returned)
    back = None
    for s in range(0, n_experts, 4):
        four = jnp.concatenate([r[...] for r in returned[s : s + 4]], axis=0)
        pick = (lax.broadcasted_iota(jnp.int32, (rows, 4 * cap), 1) + s * cap == target[...]).astype(BF)
        part = dot(pick, four)
        back = part if back is None else back + part
    out[...] = (residual[...].astype(F32) + gate_prob[...] * back).astype(BF)


def on_device(
    tokens,
    queries,
    keys,
    values,
    lengths,
    out_proj,
    norm_gain,
    expert_ids,
    gate_prob,
    w_gate,
    w_up,
    w_down,
):
    rows = tokens.shape[1]
    width = tokens.shape[2]
    heads = queries.shape[2] // HEAD
    n_ctx = lax.axis_size("ctx")
    n_ep = lax.axis_size("ep")
    me = lax.axis_index("ctx")
    y, z = lax.rem(me, Y_SIZE), lax.div(me, Y_SIZE)
    part = lax.axis_index("ep")
    y_groups = [[a * Y_SIZE + b for b in range(Y_SIZE)] for a in range(n_ctx // Y_SIZE)]

    def y_shift(array, by):
        return lax.ppermute(
            array, "ctx", [(a * Y_SIZE + b, a * Y_SIZE + (b + by) % Y_SIZE) for a in range(Z_SIZE) for b in range(Y_SIZE)]
        )

    def z_shift(array, by):
        return lax.ppermute(array, "ctx", [(i, (i + by * Y_SIZE) % n_ctx) for i in range(n_ctx)])

    def core_swap(array):
        return lax.ppermute(array, "ep", [(i, i ^ 1) for i in range(n_ep)])

    pair = jnp.concatenate([keys[0], values[0].T], axis=1)
    half = width // 2
    out_proj, pair = lax.optimization_barrier((out_proj, pair))
    mine = lax.dynamic_slice_in_dim(out_proj, lax.rem(part, 2) * half, half, 1)
    across = z_shift(mine, Z_SIZE // 2)
    row = jnp.stack([mine] + [y_shift(mine, -s) for s in range(1, Y_SIZE)])
    row, across = lax.optimization_barrier((row, across))
    opposite = jnp.stack([across] + [y_shift(across, -s) for s in range(1, Y_SIZE)])
    up, down = [row], [row]
    for _ in range(2):
        up.append(z_shift(up[-1], 1))
        down.append(z_shift(down[-1], -1))

    one_up = z_shift(pair, 1)
    to_after = jnp.arange(Y_SIZE, dtype=jnp.int32)[:, None, None] > y
    two_up = z_shift(one_up, 1)
    to_after = to_after[:, None]
    payload = jnp.where(to_after, jnp.stack([pair, one_up])[None], jnp.stack([one_up, two_up])[None])
    payload, opposite = lax.optimization_barrier((payload, opposite))
    recv = lax.all_to_all(payload, "ctx", 0, 0, axis_index_groups=y_groups)

    info = jnp.stack([me, part]).astype(jnp.int32)
    smem = pl.BlockSpec(memory_space=pltpu.SMEM)
    vmem = pl.BlockSpec(memory_space=pltpu.VMEM)
    anywhere = pl.BlockSpec(memory_space=pl.ANY)
    state = (
        jax.ShapeDtypeStruct((heads, HEAD + EXTRA, rows), F32),
        jax.ShapeDtypeStruct((heads, 1, rows), F32),
    )
    q_room = pltpu.VMEM((rows, width), BF)
    acc_room, max_room = [pltpu.VMEM(s.shape, s.dtype) for s in state]
    acc_a, max_a = call(
        near_body,
        state,
        "near",
        14,
        in_specs=[smem, smem, anywhere, vmem, anywhere],
        out_specs=(vmem, vmem),
        scratch_shapes=[q_room, pltpu.VMEM(payload.shape[1:], BF), pltpu.SemaphoreType.DMA((2,))],
        cost_estimate=cost(6e9, 6e6),
    )(info, lengths, queries[0], pair, payload)
    acc_b, max_b = call(
        mid_body,
        state,
        "mid",
        14,
        in_specs=[smem, smem, anywhere, vmem],
        out_specs=(vmem, vmem),
        scratch_shapes=[q_room, pltpu.SemaphoreType.DMA],
        cost_estimate=cost(6e9, 6e6),
    )(info, lengths, queries[0], recv)
    held_up, held_down = up[-1], down[-1]
    up.append(z_shift(held_up, 1))
    down.append(z_shift(held_down, -1))
    own_pieces = up + down[1:] + [opposite]
    up_2, down_2, swap_4, max_b = lax.optimization_barrier((up[2], down[2], opposite, max_b))
    target_across, target_down = call(
        lambda *refs: slots_body(n_ep * w_gate.shape[0], CAP, *refs),
        (jax.ShapeDtypeStruct((1, rows), jnp.int32), jax.ShapeDtypeStruct((rows, 1), jnp.int32)),
        "slots",
        8,
        in_specs=[smem, vmem, vmem],
        out_specs=(vmem, vmem),
    )(info, expert_ids[:, :, 0], expert_ids[0])
    up_0, up_1, down_1, max_a, target_across = lax.optimization_barrier((up[0], up[1], down[1], max_a, target_across))
    ready = [up_0, up_1, up_2, up[3], down_1, down_2, down[3], swap_4]
    other_pieces = [core_swap(piece) for piece in ready]
    attn = call(
        far_body,
        jax.ShapeDtypeStruct((rows, width), BF),
        "far",
        20,
        in_specs=[smem, smem, anywhere, vmem, anywhere, vmem, anywhere, vmem],
        out_specs=vmem,
        scratch_shapes=[q_room, acc_room, max_room, acc_room, acc_room, q_room, pltpu.SemaphoreType.DMA((3,))],
        cost_estimate=cost(8e9, 8e6),
    )(info, lengths, queries[0], recv, acc_a, max_a, acc_b, max_b)


    chunk = jax.ShapeDtypeStruct((CAP, width), BF)
    n_pieces = len(own_pieces)
    residual, *outgoing = call(
        project_body,
        (jax.ShapeDtypeStruct((rows, width), BF),) + (chunk,) * n_ep,
        "project",
        14,
        in_specs=[smem] + [vmem] * (2 * n_pieces + 4),
        out_specs=(vmem,) * (1 + n_ep),
        cost_estimate=cost(2.6e9, 1.4e7),
    )(info, attn, *own_pieces, *other_pieces, tokens[0], norm_gain[None, :], target_across)

    def partner(array, s):
        return lax.ppermute(array, "ep", [(i, i ^ s) for i in range(n_ep)])

    tile = 256
    ffe = w_gate.shape[2]

    def experts(members, name):
        n = len(members)
        outs = call(
            lambda *refs: expert_body(n, *refs),
            (chunk,) * n,
            name,
            24,
            in_specs=[vmem] * n + [anywhere] * 3,
            out_specs=(vmem,) * n,
            scratch_shapes=[
                pltpu.VMEM((n * CAP, width), BF),
                pltpu.VMEM((ffe // tile, width, tile), BF),
                pltpu.VMEM((ffe // tile, width, tile), BF),
                pltpu.VMEM((ffe, width), BF),
                pltpu.VMEM((n * CAP, ffe), BF),
                pltpu.SemaphoreType.DMA((2 * (ffe // tile) + 1,)),
            ],
            cost_estimate=cost(n * CAP * 6 * width * ffe, 1e7),
        )(*[incoming[s] for s in members], w_gate[0], w_up[0], w_down[0])
        answers.update(zip(members, outs))

    answers = {}
    incoming = {s: partner(outgoing[s], s) for s in (4, 5, 2, 3, 6, 7, 1)}
    incoming[0] = outgoing[0]
    experts((0, 1), "experts_self")
    incoming[4], answers[0] = lax.optimization_barrier((incoming[4], answers[0]))
    experts((4, 5), "experts_far")
    experts((2, 3, 6, 7), "experts_near")
    returned = [answers[0] if s == 0 else partner(answers[s], s) for s in range(n_ep)]

    layer_out = call(
        combine_body,
        jax.ShapeDtypeStruct((rows, width), BF),
        "combine",
        14,
        in_specs=[vmem] * (n_ep + 3),
        out_specs=vmem,
    )(*returned, residual, gate_prob[0], target_down)
    return layer_out[None]


def solution(mesh):
    placed = (
        P("ep", "ctx", None),
        P("ep", "ctx", None),
        P("ep", "ctx", None),
        P("ep", "ctx", None),
        P("ep", None),
        P("ctx", None),
        P(),
        P("ep", "ctx", None),
        P("ep", "ctx", None),
        P("ep", None, None),
        P("ep", None, None),
        P("ep", None, None),
    )
    return jax.shard_map(
        on_device, mesh=mesh, in_specs=placed, out_specs=P("ep", "ctx", None), check_vma=False
    )
```
